128 devices in a mesh: seq: 16 (over y, x), head: 8 (over z, core).
Axes of the slice: x: 4, y: 4, z: 4, core: 2. Of those that a mesh axis runs over, the one named last changes fastest.
Arguments:
- hidden_in: float32 [2, 2048, 1536], P(None, 'seq'), may hold values from -6 to 6
- cotangent: float32 [2, 2048, 1536], P(None, 'seq'), may hold values from -6 to 6
- norm_gain: float32 [2, 1536], replicated, may hold values from 0.5 to 1.5
- inner_weight: bfloat16 [2, 1536, 2, 3072], P(None, None, None, 'head'), may hold values from -0.15625 to 0.15625
- state_weight: bfloat16 [2, 1536, 256], replicated, may hold values from -0.15625 to 0.15625
- step_weight: bfloat16 [2, 1536, 48], P(None, None, 'head'), may hold values from -0.15625 to 0.15625
- conv_weight: float32 [2, 4, 3072], P(None, None, 'head'), may hold values from -3 to 3
- conv_bias: float32 [2, 3072], P(None, 'head'), may hold values from -3 to 3
- conv_state_weight: float32 [2, 4, 256], replicated, may hold values from -3 to 3
- conv_state_bias: float32 [2, 256], replicated, may hold values from -3 to 3
- step_bias: float32 [2, 48], P(None, 'head'), may hold values from -6 to -2
- decay_log: float32 [2, 48], P(None, 'head'), may hold values from -3 to 1
- skip_gain: float32 [2, 48], P(None, 'head'), may hold values from 0.5 to 1.5
- mixer_gain: float32 [2, 3072], P(None, 'head'), may hold values from 0.5 to 1.5
- output_weight: bfloat16 [2, 1536, 3072], P(None, None, 'head'), may hold values from -0.109375 to 0.109375
Outputs:
- hidden_out: float32 [2, 2048, 1536], P(None, 'seq')
- hidden_grad: float32 [2, 2048, 1536], P(None, 'seq')
- norm_gain_grad: float32 [2, 1536], replicated
- inner_weight_grad: float32 [2, 1536, 2, 3072], P(None, 'seq', None, 'head')
- state_weight_grad: float32 [2, 1536, 256], P(None, 'seq')
- step_weight_grad: float32 [2, 1536, 48], P(None, 'seq', 'head')
- conv_weight_grad: float32 [2, 4, 3072], P(None, None, 'head')
- conv_bias_grad: float32 [2, 3072], P(None, 'head')
- conv_state_weight_grad: float32 [2, 4, 256], replicated
- conv_state_bias_grad: float32 [2, 256], replicated
- step_bias_grad: float32 [2, 48], P(None, 'head')
- decay_log_grad: float32 [2, 48], P(None, 'head')
- skip_gain_grad: float32 [2, 48], P(None, 'head')
- mixer_gain_grad: float32 [2, 3072], P(None, 'head')
- output_weight_grad: float32 [2, 1536, 3072], P(None, 'seq', 'head')
The draws below stay inside these ranges and needn't reach their ends.
All inputs are finite; a program needn't handle non-finite values.
Results may differ from the reference program's by a relative error of at most 0.012.
Values sent between devices are 32-bit elements; how exact they have to be, the bound alone decides.
A program may use at most 128 MiB of HBM per device.

```python
import math
from functools import partial
import jax
import jax.numpy as jnp
from jax import lax

D = 1536
H = 48
P_SIZE = 64
N = 128
K = 4
LAYERS = 2
SEQS = 2
E = 3072
LENGTH = 2048


def block_scale(stream_key, dims, split, least, largest):
    factor_of, own = 1.0, jax.random.fold_in(stream_key, 6)
    for axis_at, parts in split:
        draws = jnp.exp(jax.random.uniform(jax.random.fold_in(own, axis_at), (parts,), jnp.float32, least / len(split), largest / len(split)))
        factor_of = factor_of * jnp.repeat(draws, dims[axis_at] // parts).reshape([-1 if axis == axis_at else 1 for axis in range(len(dims))])
    return factor_of


def gaussian(own_key, dims, scale, reach, shards=(), kind=jnp.bfloat16):
    entries = jax.random.normal(own_key, dims, jnp.float32) * scale
    if len(shards) > 0:
        entries = block_scale(own_key, dims, shards, -0.22, 0.18) * entries
    return jnp.clip(entries, min=-reach, max=reach).astype(kind)


def setup_inputs(seed: int = 0) -> dict:
    arg_keys = jax.random.split(jax.random.key(seed), 16)
    return {
        "hidden_in": gaussian(arg_keys[0], (SEQS, LENGTH, D), 1.0, 6.0, ((1, 16),), jnp.float32),
        "cotangent": gaussian(arg_keys[1], (SEQS, LENGTH, D), 1.0, 6.0, ((1, 16),), jnp.float32),
        "norm_gain": jnp.clip(1.0 + 0.1 * jax.random.normal(arg_keys[2], (LAYERS, D), jnp.float32), 0.5, 1.5),
        "inner_weight": gaussian(arg_keys[3], (LAYERS, D, 2, E), D ** -0.5, 0.15625, ((3, 8),)),
        "state_weight": gaussian(arg_keys[4], (LAYERS, D, 2 * N), D ** -0.5, 0.15625),
        "step_weight": gaussian(arg_keys[5], (LAYERS, D, H), D ** -0.5, 0.15625, ((2, 8),)),
        "conv_weight": gaussian(arg_keys[6], (LAYERS, K, E), K ** -0.5, 3.0, ((2, 8),), jnp.float32),
        "conv_bias": gaussian(arg_keys[7], (LAYERS, E), 0.5, 3.0, ((1, 8),), jnp.float32),
        "conv_state_weight": gaussian(arg_keys[8], (LAYERS, K, 2 * N), K ** -0.5, 3.0, (), jnp.float32),
        "conv_state_bias": gaussian(arg_keys[9], (LAYERS, 2 * N), 0.5, 3.0, (), jnp.float32),
        "step_bias": jnp.clip(-6.0 + 4.0 * jax.random.uniform(arg_keys[10], (LAYERS, H), jnp.float32) ** block_scale(arg_keys[10], (LAYERS, H), ((1, 8),), -0.2, 0.2), -6.0, -2.0),
        "decay_log": jnp.clip(-3.0 + 4.0 * jax.random.uniform(arg_keys[11], (LAYERS, H), jnp.float32) ** block_scale(arg_keys[11], (LAYERS, H), ((1, 8),), -0.2, 0.2), -3.0, 1.0),
        "skip_gain": jnp.clip(0.5 + 1.0 * jax.random.uniform(arg_keys[12], (LAYERS, H), jnp.float32) ** block_scale(arg_keys[12], (LAYERS, H), ((1, 8),), -0.2, 0.2), 0.5, 1.5),
        "mixer_gain": jnp.clip(1.0 + 0.1 * jax.random.normal(arg_keys[13], (LAYERS, E), jnp.float32), 0.5, 1.5),
        "output_weight": gaussian(arg_keys[14], (LAYERS, D, E), E ** -0.5, 0.109375, ((2, 8),)),
    }


HIGHEST_PRECISION = lax.Precision.HIGHEST
EPSILON = 1e-05

@jax.custom_vjp
def low(v):
    return lax.optimization_barrier(v.astype(jnp.bfloat16)).astype(jnp.float32)

@jax.custom_vjp
def low_back(v):
    return v

def low_keep(v):
    return (low(v), None)

def low_pass(kept, grad):
    return (grad,)

def back_keep(v):
    return (v, None)

def back_low(kept, grad):
    return (low(grad),)
low.defvjp(low_keep, low_pass)
low_back.defvjp(back_keep, back_low)

def rms_scale(values):
    return lax.rsqrt(lax.optimization_barrier(jnp.mean(values * values, axis=-1, keepdims=True)) + EPSILON)

def conv_apply(raw_rows, previous, kernel, offset_row):
    padded = jnp.concatenate([previous, raw_rows], axis=1)
    summed = offset_row
    for offset in range(kernel.shape[0]):
        summed = summed + kernel[offset] * padded[:, offset:offset + raw_rows.shape[1]]
    return jax.nn.silu(summed)

def block_step(decay_rates, carry_state, blocks):
    xvalues, bvalues, cvalues, step_sizes = blocks
    log_decay = jnp.cumsum(step_sizes * decay_rates, axis=1)
    block_len = xvalues.shape[1]
    lower_mask = jnp.tril(jnp.ones((block_len, block_len), jnp.bool_))[None, :, :, None]
    spread = log_decay[:, :, None, :] - log_decay[:, None, :, :]
    decays = jnp.where(lower_mask, jnp.exp(jnp.where(lower_mask, spread, 0.0)), 0.0)
    scores = jnp.einsum('sqn,skn->sqk', cvalues, bvalues, precision=HIGHEST_PRECISION)
    weights = scores[:, :, :, None] * decays * step_sizes[:, None, :, :]
    within = jnp.einsum('sqkh,skhp->sqhp', weights, xvalues, precision=HIGHEST_PRECISION)
    carried = jnp.einsum('sqn,shpn->sqhp', cvalues, carry_state, precision=HIGHEST_PRECISION) * jnp.exp(log_decay)[:, :, :, None]
    ending = log_decay[:, -1]
    tail_weights = jnp.exp(ending[:, None, :] - log_decay) * step_sizes
    update = jnp.einsum('skh,skhp,skn->shpn', tail_weights, xvalues, bvalues, precision=HIGHEST_PRECISION)
    carry_state = jnp.exp(ending)[:, :, None, None] * carry_state + update
    return (carry_state, within + carried)

def run_blocks(xvalues, bvalues, cvalues, step_sizes, decay_rates, skip_heads, start_state):
    seq_count = xvalues.shape[0]
    length_all = xvalues.shape[1]
    block_len = math.gcd(length_all, 256)
    pieces = length_all // block_len

    def split_blocks(values):
        return jnp.moveaxis(values.reshape((seq_count, pieces, block_len) + values.shape[2:]), 1, 0)
    stepper = jax.checkpoint(partial(block_step, decay_rates))
    final_state, outputs = lax.scan(stepper, start_state, (split_blocks(xvalues), split_blocks(bvalues), split_blocks(cvalues), split_blocks(step_sizes)))
    merged = jnp.moveaxis(outputs, 0, 1).reshape(xvalues.shape)
    return merged + skip_heads[:, None] * xvalues

def mamba_layer(residual, params):
    gain_in, inner_matrix, state_matrix, step_matrix, conv_matrix, conv_offset, conv_state_matrix, conv_state_offset, step_offset, decay_logs, skip_heads, gain_mix, output_matrix = params
    seq_count, length_all, model_width = residual.shape
    normed = low(residual * rms_scale(residual) * gain_in)
    flat_rows = normed.reshape(seq_count * length_all, model_width)
    proj_pair = low_back(jnp.dot(flat_rows, inner_matrix.reshape(model_width, 2 * E), precision=HIGHEST_PRECISION))
    proj_state = low_back(jnp.dot(flat_rows, state_matrix, precision=HIGHEST_PRECISION))
    proj_step = low_back(jnp.dot(flat_rows, step_matrix, precision=HIGHEST_PRECISION))
    gate_raw = proj_pair[:, :E].reshape(seq_count, length_all, E)
    inner_raw = proj_pair[:, E:].reshape(seq_count, length_all, E)
    inner_conv = low(conv_apply(inner_raw, jnp.zeros((seq_count, K - 1, E), jnp.float32), conv_matrix, conv_offset))
    state_conv = low(conv_apply(proj_state.reshape(seq_count, length_all, 2 * N), jnp.zeros((seq_count, K - 1, 2 * N), jnp.float32), conv_state_matrix, conv_state_offset))
    step_sizes = jax.nn.softplus(proj_step.reshape(seq_count, length_all, H) + step_offset)
    decay_rates = -jnp.exp(decay_logs)
    start_state = jnp.zeros((seq_count, H, P_SIZE, N), jnp.float32)
    outputs = run_blocks(inner_conv.reshape(seq_count, length_all, H, P_SIZE), state_conv[:, :, :N], state_conv[:, :, N:], step_sizes, decay_rates, skip_heads, start_state)
    gated = outputs.reshape(seq_count, length_all, E) * jax.nn.silu(gate_raw)
    mixed = low(gated * rms_scale(gated) * gain_mix)
    branch = low_back(jnp.dot(mixed.reshape(seq_count * length_all, E), output_matrix.T, precision=HIGHEST_PRECISION))
    return residual + branch.reshape(seq_count, length_all, model_width)

def reference(hidden_in, cotangent, norm_gain, inner_weight, state_weight, step_weight, conv_weight, conv_bias, conv_state_weight, conv_state_bias, step_bias, decay_log, skip_gain, mixer_gain, output_weight):
    float_params = tuple((operand.astype(jnp.float32) for operand in (norm_gain, inner_weight, state_weight, step_weight, conv_weight, conv_bias, conv_state_weight, conv_state_bias, step_bias, decay_log, skip_gain, mixer_gain, output_weight)))

    def forward(residual, *params):
        for layer_idx in range(LAYERS):
            residual = mamba_layer(residual, tuple((entry[layer_idx] for entry in params)))
        return residual
    hidden_out, pullback = jax.vjp(forward, hidden_in, *float_params)
    grads = pullback(cotangent)
    return (hidden_out, grads[0], grads[1], grads[2], grads[3], grads[4], grads[5], grads[6], grads[7], grads[8], grads[9], grads[10], grads[11], grads[12], grads[13])
```

```python
from types import SimpleNamespace

from functools import partial

import jax
import jax.numpy as jnp
from jax import lax
from jax.experimental import pallas as pl
from jax.experimental.pallas import tpu as pltpu
from jax.sharding import PartitionSpec as P

MESH = pl.DeviceIdType.MESH
HIGHEST = lax.Precision.HIGHEST
EPSILON = 1e-05
F32 = jnp.float32
LOW = jnp.bfloat16

RING = 4
SEQ = 16
HEAD = 8
SEQS = 2
LOCAL = 128
ROWS = SEQS * LOCAL
WIDTH = 1536
INNER = 384
TOTAL = 3072
HEADS = 6
STATE = 128
CONV = INNER + 2 * STATE
PROJ = 2 * INNER + 2 * STATE + 128
LANES = 128
PIECE = SEQS * INNER // SEQ
OWNERS = SEQ // SEQS
GROUPS = PIECE // 16
LAYERS = 2
HALVED = LOCAL // 2
SHARE = LOCAL // HEAD
BLOCK = WIDTH // SEQ
LAG = 0
VMEM_LIMIT = 62 * 1024 * 1024


def dot(a, b, precision=None):
    return lax.dot_general(a, b, (((1,), (0,)), ((), ())), precision=precision, preferred_element_type=F32)


def dot_nt(a, b, precision=None):
    return lax.dot_general(a, b, (((1,), (1,)), ((), ())), precision=precision, preferred_element_type=F32)


def dot_tn(a, b, precision=None):
    return lax.dot_general(a, b, (((0,), (0,)), ((), ())), precision=precision, preferred_element_type=F32)


class Place:
    def __init__(self):
        self.s = lax.axis_index("seq")
        self.h = lax.axis_index("head")
        self.x, self.y = lax.rem(self.s, RING), lax.div(self.s, RING)
        self.core, self.z = lax.rem(self.h, 2), lax.div(self.h, 2)

    def seq(self, steps):
        return lax.rem(self.s + steps + SEQ, SEQ)

    def along_seq(self, steps):
        return (self.seq(steps), self.h)

    def along_head(self, steps):
        return (self.s, lax.rem(self.h + steps, HEAD))

    def partner(self):
        return (self.s, self.h + 1 - 2 * self.core)

    def x_at(self, steps):
        return lax.rem(self.x + steps + RING, RING)

    def y_at(self, steps):
        return lax.rem(self.y + steps + RING, RING)

    def z_at(self, steps):
        return lax.rem(self.z + steps + RING, RING)

    def along_x(self, steps):
        return (self.y * RING + self.x_at(steps), self.h)

    def along_y(self, steps):
        return (self.y_at(steps) * RING + self.x, self.h)

    def along_z(self, steps):
        return (self.s, self.z_at(steps) * 2 + self.core)


class Message:
    def __init__(self, copy):
        self.copy, self.out = copy, True

    def wait_recv(self):
        self.copy.wait_recv()

    def done(self):
        if self.out:
            self.copy.wait_send()
            self.out = False


class Mail:
    def __init__(self, send, recv):
        self.send, self.recv, self.sent = send, recv, []

    def copy(self, src, dst, to):
        at = len(self.sent)
        copy = pltpu.make_async_remote_copy(
            src_ref=src,
            dst_ref=dst,
            send_sem=self.send.at[at],
            recv_sem=self.recv.at[at],
            device_id=to,
            device_id_type=MESH,
        )
        copy.start()
        self.sent.append(Message(copy))
        return self.sent[-1]

    def finish(self):
        for message in self.sent:
            message.done()


def greet(peers):
    barrier = pltpu.get_barrier_semaphore()
    for peer in peers:
        pl.semaphore_signal(barrier, inc=1, device_id=peer, device_id_type=MESH)
    return barrier


def masks():
    row = lax.broadcasted_iota(jnp.int32, (LOCAL, LOCAL), 0)
    column = lax.broadcasted_iota(jnp.int32, (LOCAL, LOCAL), 1)
    return row, column


def head_lanes():
    head = lax.broadcasted_iota(jnp.int32, (LANES, INNER), 0)
    channel = lax.broadcasted_iota(jnp.int32, (LANES, INNER), 1)
    return (lax.div(channel, INNER // HEADS) == head).astype(F32)


def split_pair(pair):
    first = lax.broadcasted_iota(jnp.int32, (LOCAL, LANES), 1) < LANES // 2
    zero = jnp.zeros_like(pair)
    return jnp.concatenate([jnp.where(first, pair, zero), jnp.where(first, zero, pair)], axis=0)


def two(values, axis):
    high = values.astype(LOW)
    return jnp.concatenate([high, (values - high.astype(F32)).astype(LOW)], axis=axis)


def twice(values, axis):
    return jnp.concatenate([values, values], axis=axis)


def product_of_two(a, b):
    high, low = b[:, :STATE], b[:, STATE:]
    return dot(a, twice(high, 0)) + dot(a[:, :INNER], low)


def rms_factor(rows):
    return lax.rsqrt(jnp.mean(rows * rows, axis=-1, keepdims=True) + EPSILON)


def head_row(ref, layer):
    return jnp.concatenate([ref[layer : layer + 1, :], jnp.zeros((1, LANES - HEADS), F32)], axis=1)


def row(ref, layer):
    return ref[layer : layer + 1, :]


def seq_rows(at):
    return slice(at * LOCAL, (at + 1) * LOCAL)


def head_sum(place, mail, part, pair, half_p, half_n, near_p, near_n, whole, first_row, finalize):
    core, z = place.core, place.z
    half = SHARE // 2

    def rows(of_core, of_z, first=0, count=SHARE):
        return pl.ds(pl.multiple_of(first_row + of_core * HALVED + of_z * SHARE + first, 8), count)

    def pair_rows(of_z):
        return pl.ds(pl.multiple_of(of_z * SHARE, 8), SHARE)

    partner, above_to, below_to = place.partner(), place.along_z(1), place.along_z(-1)
    posted = []

    def post(src, dst, to):
        posted.append(mail.copy(src, dst, to))
        return posted[-1]

    swapped = {}
    for step in (2, 1, 3, 0):
        at = place.z_at(step)
        swapped[step] = post(part.at[rows(1 - core, at)], pair.at[pair_rows(at)], partner)
    yield

    def join(step):
        at = place.z_at(step)
        swapped[step].wait_recv()
        part[rows(core, at), :] += pair[pair_rows(at), :]

    join(2)
    far, above, below = place.z_at(2), place.z_at(1), place.z_at(-1)
    first, last = pl.ds(0, half), pl.ds(half, half)
    up = post(part.at[rows(core, far, 0, half)], half_p, above_to)
    down = post(part.at[rows(core, far, half, half)], half_n, below_to)
    join(1)
    near = [post(part.at[rows(core, above, half, half)], near_p.at[last], above_to)]
    join(3)
    near.append(post(part.at[rows(core, below, 0, half)], near_n.at[first], below_to))
    join(0)
    yield
    up.wait_recv()
    part[rows(core, above, 0, half), :] += half_p[...]
    near.append(post(part.at[rows(core, above, 0, half)], near_p.at[first], above_to))
    down.wait_recv()
    part[rows(core, below, half, half), :] += half_n[...]
    near.append(post(part.at[rows(core, below, half, half)], near_n.at[last], below_to))
    yield
    for message in near:
        message.wait_recv()
    mine = rows(core, z)
    whole[mine, :] = finalize(part[mine, :] + near_p[...] + near_n[...], mine)
    up = post(whole.at[mine], whole.at[mine], above_to)
    down = post(whole.at[mine], whole.at[mine], below_to)
    across = [post(whole.at[mine], whole.at[mine], partner)]
    yield
    up.wait_recv()
    piece = rows(core, below, 0, half)
    up = post(whole.at[piece], whole.at[piece], above_to)
    piece = rows(core, below)
    across.append(post(whole.at[piece], whole.at[piece], partner))
    down.wait_recv()
    piece = rows(core, above, half, half)
    down = post(whole.at[piece], whole.at[piece], below_to)
    piece = rows(core, above)
    across.append(post(whole.at[piece], whole.at[piece], partner))
    yield
    up.wait_recv()
    piece = rows(core, far, 0, half)
    across.append(post(whole.at[piece], whole.at[piece], partner))
    down.wait_recv()
    piece = rows(core, far, half, half)
    across.append(post(whole.at[piece], whole.at[piece], partner))
    yield
    for message in across:
        message.wait_recv()
    for message in posted:
        message.done()


HEAD_SUM_COPIES = 4 + 2 + 4 + 2 + 2 + 5


class Exchange:
    def __init__(self, place, r, at, reverse):
        self.place, self.r, self.at, self.reverse = place, r, at, reverse
        self.owner = lax.div(place.s, OWNERS) == at

    def to_owner(self, k):
        owner = self.at * OWNERS + k
        r, s = self.r, self.place.s
        return pltpu.make_async_remote_copy(
            src_ref=r.stage.at[owner],
            dst_ref=r.seen.at[s],
            send_sem=r.leg1_send.at[owner],
            recv_sem=r.leg1_recv.at[s],
            device_id=(owner, self.place.h),
            device_id_type=MESH,
        )

    def from_source(self, k):
        r, source = self.r, self.place.seq(k)
        return pltpu.make_async_remote_copy(
            src_ref=r.stage.at[source],
            dst_ref=r.seen.at[source],
            send_sem=r.leg1_send.at[source],
            recv_sem=r.leg1_recv.at[source],
            device_id=(source, self.place.h),
            device_id_type=MESH,
        )

    def to_device(self, k):
        r, s, to = self.r, self.place.s, self.place.seq(k)
        return pltpu.make_async_remote_copy(
            src_ref=r.turned.at[to],
            dst_ref=r.back.at[s],
            send_sem=r.leg2_send.at[to],
            recv_sem=r.leg2_recv.at[s],
            device_id=(to, self.place.h),
            device_id_type=MESH,
        )

    def from_owner(self, k):
        owner = self.at * OWNERS + k
        r = self.r
        return pltpu.make_async_remote_copy(
            src_ref=r.turned.at[owner],
            dst_ref=r.back.at[owner],
            send_sem=r.leg2_send.at[owner],
            recv_sem=r.leg2_recv.at[owner],
            device_id=(owner, self.place.h),
            device_id_type=MESH,
        )

    def each_owner(self, what):
        for k in range(OWNERS):

            @pl.when(self.at * OWNERS + k != self.place.s)
            def _(k=k):
                what(k)

    def start(self, state, decays):
        r = self.r
        for piece in range(OWNERS):
            slot = self.at * OWNERS + piece
            r.stage[slot, 0:PIECE, :] = state[piece * PIECE : (piece + 1) * PIECE]
            for group in range(GROUPS):
                head = (piece * GROUPS + group) // 4
                r.stage[slot, PIECE + group : PIECE + group + 1, :] = decays[head]
            r.stage[slot, PIECE + GROUPS : PIECE + 8, :] = jnp.zeros((8 - GROUPS, LANES), F32)
        self.each_owner(lambda k: self.to_owner(k).start())

        @pl.when(self.owner)
        def _():
            r.seen[self.place.s] = r.stage[self.place.s]

    def turn(self):
        r = self.r

        @pl.when(self.owner)
        def _():
            def landed(k, carry):
                self.from_source(k).wait_recv()
                return carry

            lax.fori_loop(1, SEQ, landed, 0)

            def hop(step, carry):
                at = SEQ - 1 - step if self.reverse else step
                for group in range(GROUPS):
                    r.turned[at, group * 16 : group * 16 + 16, :] = carry[group]
                return tuple(
                    r.seen[at, PIECE + group : PIECE + group + 1, :] * carry[group]
                    + r.seen[at, group * 16 : group * 16 + 16, :]
                    for group in range(GROUPS)
                )

            lax.fori_loop(0, SEQ, hop, tuple(jnp.zeros((16, LANES), F32) for _ in range(GROUPS)))

            def send(k, carry):
                self.to_device(k).start()
                return carry

            lax.fori_loop(1, SEQ, send, 0)
            r.back[self.place.s] = r.turned[self.place.s]

    def finish(self):
        self.each_owner(lambda k: self.from_owner(k).wait_recv())
        self.each_owner(lambda k: self.to_owner(k).wait_send())

        @pl.when(self.owner)
        def _():
            def left(k, carry):
                self.to_device(k).wait_send()
                return carry

            lax.fori_loop(1, SEQ, left, 0)

        return self.r.back[self.at * OWNERS : (self.at + 1) * OWNERS].reshape(INNER, STATE)


SMALL = 128
SMALL_PIECE = SMALL // SEQ
PART = 2 * STATE // HEAD
MISC = PART + 8
SHARED = ((11, 13), (16, 18), (21, 23), (26, 28), (31, 33), (33, 45))
HALF = BLOCK // 2
QUARTER = BLOCK // 4
CHUNKS = 3


class Program:
    def __init__(self, r):
        self.r = r
        self.place = Place()
        self.mail = Mail(r.mail_send, r.mail_recv)
        self.loads = {}
        self.sums_sent = {}
        self.stores = []


    def load(self, name, src, dst):
        copy = pltpu.make_async_copy(src, dst, self.r.load.at[len(self.loads)])
        copy.start()
        self.loads[name] = copy

    def need(self, *names):
        for name in names:
            copy = self.loads.get(name)
            if copy is not None:
                copy.wait()
                self.loads[name] = None

    def start_loads(self):
        r = self.r
        for b in range(SEQS):
            self.load((0, b), r.hidden_in.at[b], r.res.at[0, pl.ds(b * LOCAL, LOCAL)])
        for l in range(LAYERS):
            self.load((1, l), r.inner_in.at[l, 1], r.inner.at[l, 1])
            self.load((2, l), r.state_in.at[l], r.state.at[l])
            self.load((3, l), r.inner_in.at[l, 0], r.inner.at[l, 0])
            self.load((4, l), r.output_in.at[l], r.wout.at[l])
        for b in range(SEQS):
            self.load((5, b), r.cotangent_in.at[b], r.grad.at[LAYERS, pl.ds(b * LOCAL, LOCAL)])

    def put(self, source, target):
        for b in range(SEQS):
            copy = pltpu.make_async_copy(
                source.at[pl.ds(b * LOCAL, LOCAL)], target.at[b], self.r.store.at[len(self.stores)]
            )
            copy.start()
            self.stores.append(copy)

    def store(self):
        self.put(self.r.res.at[LAYERS], self.r.hidden_out)
        yield

    def head_summing(self, l, b, part, extra, whole, finalize):
        r = self.r
        pair, half_p, half_n, near_p, near_n = extra
        return head_sum(
            self.place,
            self.mail,
            part,
            pair.at[b],
            half_p.at[b],
            half_n.at[b],
            near_p.at[b],
            near_n.at[b],
            whole,
            b * LOCAL,
            finalize,
        )

    def wide(self):
        r = self.r
        return r.pair, r.half_p, r.half_n, r.near_p, r.near_n

    def last(self):
        r = self.r
        return r.last_pair, r.last_half_p, r.last_half_n, r.last_near_p, r.last_near_n

    def add_small(self, l, at, values):
        for k in range(values.shape[1] // LANES):
            self.r.small[l, at + k : at + k + 1, :] += values[:, k * LANES : (k + 1) * LANES]

    def taps(self, l, tap):
        r = self.r
        return jnp.concatenate([r.conv_weight[l, tap : tap + 1, :], r.conv_state_weight[l, tap : tap + 1, :]], axis=1)

    def decays(self, l, b):
        r = self.r
        decay = jnp.exp(r.logs[l, (b + 1) * LOCAL - 1 : (b + 1) * LOCAL, :])
        return [jnp.broadcast_to(decay[:, h : h + 1], (1, LANES)) for h in range(HEADS)]

    def forward(self, l, b):
        r, place, mail = self.r, self.place, self.mail
        here = seq_rows(b)
        gain = row(r.norm_gain, l)
        self.need((0, b))

        def norm_rows(at, carry):
            rows = pl.ds(pl.multiple_of(b * LOCAL + at * 32, 32), 32)
            values = r.res[l, rows, :]
            r.normed[l, rows, :] = (values * rms_factor(values) * gain).astype(LOW)
            return carry

        edge = mail.copy(r.res.at[l, pl.ds((b + 1) * LOCAL - 8, 8)], r.halo.at[l, b], place.along_seq(1))
        lax.fori_loop(0, LOCAL // 32, norm_rows, 0)
        self.need((1, l), (2, l))
        normed = r.normed[l, here, :]
        r.raw[l, b, 8:, :INNER] = dot(normed, r.inner[l, 1])
        r.raw[l, b, 8:, INNER:] = dot(normed, r.state[l])
        pushed = jnp.concatenate([dot_nt(normed, r.step[l]), jnp.zeros((LOCAL, LANES - HEADS), F32)], axis=1)
        pushed = pushed + head_row(r.step_bias, l)
        sizes = jax.nn.softplus(pushed)
        r.dt[l, here, :] = sizes
        r.sig[l, here, :] = jax.nn.sigmoid(pushed)
        rows, columns = masks()
        lower = (rows >= columns).astype(F32)
        rate = -jnp.exp(head_row(r.decay_log, l))
        r.logs[l, here, :] = dot(lower, sizes * rate, HIGHEST)
        yield
        edge.wait_recv()
        values = r.halo[l, b]
        borrowed = jnp.where(place.s == 0, 0.0, values * rms_factor(values) * gain).astype(LOW)
        r.raw[l, b, 0:8, :INNER] = dot(borrowed, r.inner[l, 1])
        r.raw[l, b, 0:8, INNER:] = dot(borrowed, r.state[l])
        summed = jnp.concatenate([row(r.conv_bias, l), row(r.conv_state_bias, l)], axis=1)
        for tap in range(4):
            summed = summed + self.taps(l, tap) * r.raw[l, b, 5 + tap : 5 + tap + LOCAL, :]
        r.pre[l, here, :] = summed
        r.act[l, here, :] = (summed * jax.nn.sigmoid(summed)).astype(LOW)
        lanes = head_lanes()
        ending = r.logs[l, (b + 1) * LOCAL - 1 : (b + 1) * LOCAL, :]
        tail = dot(jnp.exp(ending - r.logs[l, here, :]) * r.dt[l, here, :], lanes, HIGHEST)
        xs, bs, cs = r.act[l, here, :INNER], r.act[l, here, INNER : INNER + STATE], r.act[l, here, INNER + STATE :]
        exchange = Exchange(place, r, b, False)
        exchange.start(dot_tn(two(xs.astype(F32) * tail, 0), twice(bs, 0)), self.decays(l, b))
        yield
        self.need((3, l))
        r.gate[l, here, :] = dot(normed, r.inner[l, 0])
        scores = jnp.where(rows >= columns, dot_nt(cs, bs), 0.0)
        turned_logs = r.logs[l, here, :].T
        turned_dt = r.dt[l, here, :].T
        for p in range(HEADS // 2):
            weights = []
            for h in (2 * p, 2 * p + 1):
                fall = jnp.minimum(r.logs[l, here, h : h + 1] - turned_logs[h : h + 1, :], 0.0)
                weights.append(scores * jnp.exp(fall) * turned_dt[h : h + 1, :])
            cols = slice(p * LANES, (p + 1) * LANES)
            r.y[l, here, cols] = dot(two(jnp.concatenate(weights, axis=1), 1), twice(split_pair(xs[:, cols]), 0))
        yield
        exchange.turn()
        yield
        start = exchange.finish()
        r.s0[l, b * INNER : (b + 1) * INNER, :] = start
        grown = dot(jnp.exp(r.logs[l, here, :]), lanes, HIGHEST)
        skip = dot(head_row(r.skip_gain, l), lanes, HIGHEST)
        values = r.y[l, here, :] + dot_nt(twice(cs, 1), two(start, 1)) * grown + skip * xs.astype(F32)
        r.y[l, here, :] = values
        gates = r.gate[l, here, :]
        gated = values * (gates * jax.nn.sigmoid(gates))
        ones = jnp.ones((8, INNER), F32)
        sums = dot_nt(ones, gated * gated, HIGHEST)
        mixer = row(r.mixer_gain, l)
        self.need((4, l))
        if l == LAYERS - 1:
            self.need((5, b))
            r.grad_low[l, here, :] = r.grad[LAYERS, here, :].astype(LOW)
            dmixed = dot(r.grad_low[l, here, :], r.wout[l])
            r.dmixed[here, :] = dmixed
            inner_sums = dot_nt(ones, dmixed * mixer * gated, HIGHEST)
            first = lax.broadcasted_iota(jnp.int32, (8, LOCAL), 0) == 0
            sums = jnp.where(first, sums, inner_sums)
        r.sums[l, b] = sums
        r.sums_seen[l, b, place.h] = sums
        self.sums_sent[l, b] = [
            mail.copy(r.sums.at[l, b], r.sums_seen.at[l, b, place.h], place.along_head(k)) for k in range(1, HEAD)
        ]
        r.gated[here, :] = gated
        yield
        self.over_head(l, b)
        r.mixed[l, here, :] = (r.gated[here, :] * r.factor[l, here, :][:, :1] * mixer).astype(LOW)
        part = r.part if l < LAYERS - 1 else r.last_part
        part[here, :] = dot_nt(r.mixed[l, here, :], r.wout[l])

    def over_head(self, l, b):
        r = self.r
        for message in self.sums_sent[l, b]:
            message.wait_recv()
        sums = r.sums_seen[l, b, 0]
        for k in range(1, HEAD):
            sums = sums + r.sums_seen[l, b, k]
        columns = jnp.concatenate([sums, jnp.zeros((LOCAL - 8, LOCAL), F32)], axis=0).T
        factor = lax.rsqrt(columns[:, 0:1] / TOTAL + EPSILON)
        r.factor[l, seq_rows(b), :] = jnp.broadcast_to(factor, (LOCAL, LANES))
        r.means[seq_rows(b), :] = jnp.broadcast_to(columns[:, 1:2] * factor / TOTAL, (LOCAL, LANES))

    def forward_sum(self, l, b):
        r = self.r

        def finalize(total, mine):
            return r.res[l, mine, :] + total

        if l < LAYERS - 1:
            return self.head_summing(l, b, r.part, self.wide(), r.res.at[l + 1], finalize)
        return self.head_summing(l, b, r.last_part, self.last(), r.res.at[l + 1], finalize)

    def backward(self, l, b):
        r, place, mail = self.r, self.place, self.mail
        here = seq_rows(b)
        lanes = head_lanes()
        rows, columns = masks()
        mixer = row(r.mixer_gain, l)
        skip = dot(head_row(r.skip_gain, l), lanes, HIGHEST)
        xs, bs, cs = r.act[l, here, :INNER], r.act[l, here, INNER : INNER + STATE], r.act[l, here, INNER + STATE :]
        if l == LAYERS - 1:
            dmixed, means = r.dmixed[here, :], r.means[here, :][:, :1]
        else:
            low = r.grad[l + 1, here, :].astype(LOW)
            r.grad_low[l, here, :] = low
            dmixed = dot(low, r.wout[l])
            branch = r.res[l + 1, here, :] - r.res[l, here, :]
            means = jnp.sum(low.astype(F32) * branch, axis=-1, keepdims=True) / TOTAL
        factor = r.factor[l, here, :][:, :1]
        gates, values = r.gate[l, here, :], r.y[l, here, :]
        opened = jax.nn.sigmoid(gates)
        silu = gates * opened
        q = values * silu * factor
        self.add_small(l, 0, jnp.sum(dmixed * q, axis=0, keepdims=True))
        dgated = factor * (dmixed * mixer - q * means)
        dvalues = dgated * silu
        r.dy[here, :] = dvalues
        r.dproj[l, here, :INNER] = (dgated * values * opened * (1.0 + gates * (1.0 - opened))).astype(LOW)
        self.add_small(l, 3, jnp.sum(dvalues * xs.astype(F32), axis=0, keepdims=True))
        grown = dot(jnp.exp(r.logs[l, here, :]), lanes, HIGHEST)
        scaled = two(grown * dvalues, 1)
        exchange = Exchange(place, r, b, True)
        exchange.start(dot_tn(two(grown * dvalues, 0), twice(cs, 0)), self.decays(l, b))
        yield
        inside = (rows >= columns).astype(F32)
        scores = dot_nt(cs, bs) * inside
        turned_logs = r.logs[l, here, :].T
        turned_dt = r.dt[l, here, :].T
        dscores = jnp.zeros((LOCAL, LOCAL), F32)
        row_sums, column_sums = [], []
        for p in range(HEADS // 2):
            cols = slice(p * LANES, (p + 1) * LANES)
            dys = two(split_pair(r.dy[here, cols]), 1)
            both = dot_nt(dys, twice(xs[:, cols], 1))
            weights = []
            for k in range(2):
                h = 2 * p + k
                fall = jnp.exp(jnp.minimum(r.logs[l, here, h : h + 1] - turned_logs[h : h + 1, :], 0.0))
                steps = turned_dt[h : h + 1, :]
                weights.append(scores * fall * steps)
                moved = both[k * LOCAL : (k + 1) * LOCAL] * fall
                dscores += moved * steps
                moved = moved * scores
                column_sums.append(jnp.sum(moved, axis=0, keepdims=True))
                row_sums.append(jnp.sum(moved * steps, axis=1, keepdims=True))
            weights = two(jnp.concatenate(weights, axis=0), 0)
            high, low = dys[:, :LANES], dys[:, LANES:]
            r.dact[here, cols] = dot_tn(weights, twice(high, 0)) + dot_tn(weights[:SEQS * LOCAL], low)
        dscores = dscores * inside
        start = two(r.s0[l, b * INNER : (b + 1) * INNER, :], 1)
        r.dact[here, INNER : INNER + STATE] = dot_tn(two(dscores, 0), twice(cs, 0))
        r.dact[here, INNER + STATE :] = dot(two(dscores, 1), twice(bs, 0)) + product_of_two(scaled, start)
        carried = dot_nt(twice(cs, 1), start)
        from_start = dot_nt(carried * r.dy[here, :], lanes, HIGHEST) * jnp.exp(r.logs[l, here, :])
        by_column = jnp.concatenate(column_sums + [jnp.zeros((LOCAL - HEADS, LOCAL), F32)], axis=0).T
        by_row = jnp.concatenate(row_sums + [jnp.zeros((LOCAL, LANES - HEADS), F32)], axis=1)
        r.dlogs[b, 0] = by_row - by_column * r.dt[l, here, :] + from_start
        r.dlogs[b, 1] = by_column
        yield
        exchange.turn()
        yield
        upper = (rows <= columns).astype(F32)
        strict = (rows > columns).astype(F32)
        ending = r.logs[l, (b + 1) * LOCAL - 1 : (b + 1) * LOCAL, :]
        tail = jnp.exp(ending - r.logs[l, here, :])
        tail_dt = dot(tail * r.dt[l, here, :], lanes, HIGHEST)
        ends = exchange.finish()
        ends_two = two(ends, 1)
        reach = dot_nt(twice(bs, 1), ends_two)
        xs = xs.astype(F32)
        pulled = dot_nt(xs * reach, lanes, HIGHEST) * tail
        r.dact[here, :INNER] += tail_dt * reach + skip * r.dy[here, :]
        r.dact[here, INNER : INNER + STATE] += product_of_two(two(xs * tail_dt, 1), ends_two)
        ones = jnp.ones((8, LANES), F32)
        starts = r.s0[l, b * INNER : (b + 1) * INNER, :]
        overlap = dot_nt(dot_nt(ones, ends * starts, HIGHEST), lanes, HIGHEST)[:1]
        dt = r.dt[l, here, :]
        dlas = (
            dot(upper, r.dlogs[b, 0], HIGHEST) + dot(strict, pulled * dt, HIGHEST) + overlap * jnp.exp(ending)
        )
        rate = -jnp.exp(head_row(r.decay_log, l))
        dstep = (r.dlogs[b, 1] + pulled + dlas * rate) * r.sig[l, here, :]
        r.dproj[l, here, INNER + CONV :] = dstep.astype(LOW)
        before = r.pre[l, here, :]
        opened = jax.nn.sigmoid(before)
        dbefore = r.dact[here, :] * opened * (1.0 + before * (1.0 - opened))
        r.dpre[b, 0:LOCAL, :] = dbefore
        r.edge[l, b] = dbefore[0:8]
        edge = mail.copy(r.edge.at[l, b], r.edge_seen.at[l, b], place.along_seq(-1))
        self.add_small(l, 6, jnp.sum(dstep, axis=0, keepdims=True))
        self.add_small(l, 7, jnp.sum(dlas * dt, axis=0, keepdims=True) * rate)
        self.add_small(l, 8, jnp.sum(dbefore, axis=0, keepdims=True))
        for tap in range(4):
            shifted = r.raw[l, b, 5 + tap : 5 + tap + LOCAL, :]
            self.add_small(l, 13 + 5 * tap, jnp.sum(dbefore * shifted, axis=0, keepdims=True))
        r.part[here, :] = dot_nt(r.dproj[l, here, :INNER], r.inner[l, 0]) + dot(
            r.dproj[l, here, INNER + CONV : INNER + CONV + HEADS], r.step[l]
        )
        yield
        edge.wait_recv()
        r.dpre[b, LOCAL:, :] = jnp.where(place.s == SEQ - 1, 0.0, r.edge_seen[l, b])
        draw = jnp.zeros((LOCAL, CONV), F32)
        for tap in range(4):
            draw += self.taps(l, tap) * r.dpre[b, 3 - tap : 3 - tap + LOCAL, :]
        r.dproj[l, here, INNER : INNER + CONV] = draw.astype(LOW)
        r.state_part[l, :, here] = draw[:, INNER:].T
        r.part[here, :] += dot_nt(r.dproj[l, here, INNER : 2 * INNER], r.inner[l, 1]) + dot_nt(
            r.dproj[l, here, 2 * INNER : INNER + CONV], r.state[l]
        )

    def backward_sum(self, l, b):
        r = self.r

        def finalize(dnormed, mine):
            rows = r.res[l, mine, :]
            factor = rms_factor(rows)
            u = rows * factor
            self.add_small(l, 33, jnp.sum(dnormed * u, axis=0, keepdims=True))
            du = dnormed * row(r.norm_gain, l)
            return r.grad[l + 1, mine, :] + factor * (du - u * jnp.mean(du * u, axis=-1, keepdims=True))

        return self.head_summing(l, b, r.part, self.wide(), r.grad.at[l], finalize)


    def weight_chunk(self, l, chunk):
        r, place, mail = self.r, self.place, self.mail
        own, flows = r.own, (0, 1)

        def blocks(flow, at, first, count):
            rows = pl.ds(flow * HALF + first, count)
            if flow == 0:
                return (chunk, slice(None), at, rows, slice(None))
            return (chunk, at, slice(None), rows, slice(None))

        def move(flow, steps):
            return place.along_x(steps) if flow == 0 else place.along_y(steps)

        def at_of(flow, steps):
            return place.x_at(steps) if flow == 0 else place.y_at(steps)

        def slot(flow):
            return chunk * 2 + flow

        posted = []

        def post(src, dst, to):
            posted.append(mail.copy(src, dst, to))
            return posted[-1]

        for k in range(RING):
            cols = slice(k * INNER, (k + 1) * INNER)
            if chunk == 0:
                value = dot_tn(r.grad_low[l, :, cols], r.mixed[l])
            else:
                value = dot_tn(r.normed[l, :, cols], r.dproj[l, :, (chunk - 1) * INNER : chunk * INNER])
            own[chunk, k] = value.reshape(RING, BLOCK, INNER)
        first, last = pl.ds(0, QUARTER), pl.ds(QUARTER, QUARTER)
        distant, near = {}, {}

        def parts(ref, flow, rows):
            return ref.at[slot(flow), :, rows]

        for flow in flows:
            far = at_of(flow, 2)
            distant[flow] = (
                post(own.at[blocks(flow, far, 0, QUARTER)], r.a1p.at[slot(flow)], move(flow, 1)),
                post(own.at[blocks(flow, far, QUARTER, QUARTER)], r.a1n.at[slot(flow)], move(flow, -1)),
            )
        for flow in flows:
            up, down = at_of(flow, 1), at_of(flow, -1)
            near[flow] = [
                post(own.at[blocks(flow, up, QUARTER, QUARTER)], parts(r.a2p, flow, last), move(flow, 1)),
                post(own.at[blocks(flow, down, 0, QUARTER)], parts(r.a2n, flow, first), move(flow, -1)),
            ]
        yield
        for flow in flows:
            up, down = at_of(flow, 1), at_of(flow, -1)
            for message in distant[flow]:
                message.wait_recv()
            own[blocks(flow, up, 0, QUARTER)] += r.a1p[slot(flow)]
            own[blocks(flow, down, QUARTER, QUARTER)] += r.a1n[slot(flow)]
            near[flow] += [
                post(own.at[blocks(flow, up, 0, QUARTER)], parts(r.a2p, flow, first), move(flow, 1)),
                post(own.at[blocks(flow, down, QUARTER, QUARTER)], parts(r.a2n, flow, last), move(flow, -1)),
            ]
        yield
        for flow in flows:
            k = slot(flow)
            for message in near[flow]:
                message.wait_recv()
            r.asum[k] = own[blocks(flow, at_of(flow, 0), 0, HALF)] + r.a2p[k] + r.a2n[k]
            other = 1 - flow
            far, up, down = at_of(other, 2), at_of(other, 1), at_of(other, -1)
            distant[flow] = (
                post(r.asum.at[k, far, first], r.a3p.at[k], move(other, 1)),
                post(r.asum.at[k, far, last], r.a3n.at[k], move(other, -1)),
            )
            near[flow] = [
                post(r.asum.at[k, up, last], r.a4p.at[k, last], move(other, 1)),
                post(r.asum.at[k, down, first], r.a4n.at[k, first], move(other, -1)),
            ]
        yield
        for flow in flows:
            k = slot(flow)
            other = 1 - flow
            up, down = at_of(other, 1), at_of(other, -1)
            for message in distant[flow]:
                message.wait_recv()
            r.asum[k, up, 0:QUARTER] += r.a3p[k]
            r.asum[k, down, QUARTER:HALF] += r.a3n[k]
            near[flow] += [
                post(r.asum.at[k, up, first], r.a4p.at[k, first], move(other, 1)),
                post(r.asum.at[k, down, last], r.a4n.at[k, last], move(other, -1)),
            ]
        yield
        for flow in flows:
            k = slot(flow)
            for message in near[flow]:
                message.wait_recv()
            value = r.asum[k, at_of(1 - flow, 0)] + r.a4p[k] + r.a4n[k]
            rows = slice(flow * HALF, (flow + 1) * HALF)
            if chunk == 0:
                r.output_grad[l, rows, :] = value
            else:
                r.pair_grad[l, chunk - 1, rows, :] = value
        for message in posted:
            message.done()

    def spread(self, src, dst, l, sems, slots):
        place = self.place

        def message(k):
            to = place.seq(k)
            return pltpu.make_async_remote_copy(
                src_ref=src(to) if slots is None else src.at[to] if slots else src,
                dst_ref=dst.at[place.s],
                send_sem=sems[0].at[l, k],
                recv_sem=sems[1].at[l, k],
                device_id=(to, place.h),
                device_id_type=MESH,
            )

        def each(what):
            def body(k, carry):
                what(message(k))
                return carry

            return lambda: lax.fori_loop(1, SEQ, body, 0)

        each(lambda m: m.start())()
        return each(lambda m: m.wait_recv()), each(lambda m: m.wait_send())

    def to_heads(self, src, dst, slots):
        place, mail = self.place, self.mail
        sent = []
        for k in range(1, HEAD):
            to = lax.rem(place.h + k, HEAD)
            piece = src.at[pl.ds(pl.multiple_of(to * PART, PART), PART)] if slots else src
            sent.append(mail.copy(piece, dst.at[place.h], (place.s, to)))
        return sent

    def state_weights(self, l):
        r, place = self.r, self.place
        sent = self.to_heads(r.state_part.at[l], r.state_seen.at[l], True)
        yield
        total = r.state_part[l, pl.ds(pl.multiple_of(place.h * PART, PART), PART), :]
        for k in range(1, HEAD):
            sent[k - 1].wait_recv()
        for k in range(1, HEAD):
            total = total + r.state_seen[l, lax.rem(place.h + k, HEAD)]
        steps = r.dproj[l, :, INNER + CONV :].astype(F32).T[0:8]
        both = jnp.concatenate([total, steps], axis=0).astype(LOW)
        for k in range(RING):
            product = dot(both, r.normed[l, :, k * INNER : (k + 1) * INNER])
            for j in range(RING):
                owner = k * RING + j
                r.misc[l, owner, :, 0:BLOCK] = product[:, j * BLOCK : (j + 1) * BLOCK]
        r.misc_seen[l, place.s] = r.misc[l, place.s]
        scattered = self.spread(r.misc.at[l], r.misc_seen.at[l], l, (r.scatter_send, r.scatter_recv), True)
        yield
        scattered[0]()
        total = r.misc_seen[l, 0]
        for k in range(1, SEQ):
            total = total + r.misc_seen[l, k]
        r.step_grad[l] = total[PART:]
        r.shared[l] = total[0:PART]
        r.state_grad[l, place.h] = total[0:PART]
        sent = self.to_heads(r.shared.at[l], r.shared_seen.at[l], False)
        yield
        for message in sent:
            message.wait_recv()
        for k in range(1, HEAD):
            at = lax.rem(place.h + k, HEAD)
            r.state_grad[l, at] = r.shared_seen[l, at]
        scattered[1]()

    def small_sums(self, l):
        r, place = self.r, self.place
        r.tiny_seen[l, place.s] = r.small[l, pl.ds(pl.multiple_of(place.s * SMALL_PIECE, 8), SMALL_PIECE), :]

        def piece(to):
            return r.small.at[l, pl.ds(pl.multiple_of(to * SMALL_PIECE, 8), SMALL_PIECE)]

        scattered = self.spread(piece, r.tiny_seen.at[l], l, (r.tiny_send, r.tiny_recv), None)
        yield
        scattered[0]()
        total = r.tiny_seen[l, 0]
        for k in range(1, SEQ):
            total = total + r.tiny_seen[l, k]
        r.tiny[l] = total
        sent = self.to_heads(r.tiny.at[l], r.tiny_heads.at[l], False)
        yield
        for message in sent:
            message.wait_recv()
        over_head = total
        for k in range(1, HEAD):
            over_head = over_head + r.tiny_heads[l, lax.rem(place.h + k, HEAD)]
        at = lax.broadcasted_iota(jnp.int32, (SMALL_PIECE, LANES), 0) + place.s * SMALL_PIECE
        joint = at < 0
        for low, high in SHARED:
            joint = joint | ((at >= low) & (at < high))
        r.small_seen[l, place.s] = jnp.where(joint, over_head, total)
        gathered = self.spread(
            r.small_seen.at[l, place.s], r.small_seen.at[l], l, (r.gather_send, r.gather_recv), False
        )
        yield
        gathered[0]()
        r.small_out[l] = r.small_seen[l]
        gathered[1]()
        scattered[1]()


FORWARD, FORWARD_SUM, FORWARD_DONE, BACKWARD, BACKWARD_SUM, BACKWARD_DONE = range(6)


def chain(program, b):
    for l in range(LAYERS):
        for step, _ in enumerate(program.forward(l, b)):
            yield FORWARD, l, step
        if l < LAYERS - 1:
            for step, _ in enumerate(program.forward_sum(l, b)):
                yield FORWARD_SUM, l, step
        else:
            yield FORWARD_DONE, l, 0
    for l in reversed(range(LAYERS)):
        for step, _ in enumerate(program.backward(l, b)):
            yield BACKWARD, l, step
        for step, _ in enumerate(program.backward_sum(l, b)):
            yield BACKWARD_SUM, l, step
        yield BACKWARD_DONE, l, 0


def last(b):
    return Program.forward_sum, LAYERS - 1, b


def chunk(l, k):
    return Program.weight_chunk, l, k


def state(l):
    return Program.state_weights, l


def small(l):
    return Program.small_sums, l


STORE = (Program.store,)

BEHIND = {
    (FORWARD_DONE, 1, 0, 0): (last(0),),
    (FORWARD_DONE, 1, 0, 1): (last(1),),
    (BACKWARD, 1, 0, 0): (last(0),),
    (BACKWARD, 1, 0, 1): (last(1),),
    (BACKWARD, 1, 1, 0): (last(0),),
    (BACKWARD, 1, 1, 1): (last(1),),
    (BACKWARD, 1, 2, 0): (last(0),),
    (BACKWARD, 1, 2, 1): (last(1), chunk(1, 0)),
    (BACKWARD, 1, 3, 0): (last(0),),
    (BACKWARD, 1, 3, 1): (last(1), chunk(1, 0), chunk(1, 1)),
    (BACKWARD_SUM, 1, 0, 0): (last(0),),
    (BACKWARD_SUM, 1, 0, 1): (last(1), state(1), chunk(1, 0), chunk(1, 1), chunk(1, 2)),
    (BACKWARD_SUM, 1, 1, 0): (last(0),),
    (BACKWARD_SUM, 1, 1, 1): (last(1), chunk(1, 1)),
    (BACKWARD_SUM, 1, 2, 1): (state(1), chunk(1, 0), chunk(1, 2)),
    (BACKWARD_SUM, 1, 3, 1): (chunk(1, 1), chunk(1, 0)),
    (BACKWARD_SUM, 1, 4, 1): (chunk(1, 1), chunk(1, 2)),
    (BACKWARD_SUM, 1, 5, 1): (chunk(1, 2), chunk(1, 2), state(1)),
    (BACKWARD_DONE, 1, 0, 1): (STORE,),
    (BACKWARD, 0, 1, 1): (state(1), small(1)),
    (BACKWARD, 0, 2, 1): (chunk(0, 0),),
    (BACKWARD, 0, 3, 1): (chunk(0, 0), chunk(0, 1)),
    (BACKWARD_SUM, 0, 0, 1): (state(0), chunk(0, 0), chunk(0, 1), chunk(0, 2), small(1)),
    (BACKWARD_SUM, 0, 1, 1): (state(0), chunk(0, 1)),
    (BACKWARD_SUM, 0, 2, 1): (chunk(0, 0), chunk(0, 2), small(1)),
    (BACKWARD_SUM, 0, 3, 1): (small(0), state(0), chunk(0, 1), chunk(0, 0)),
    (BACKWARD_SUM, 0, 4, 1): (small(0), chunk(0, 2), chunk(0, 1)),
    (BACKWARD_SUM, 0, 5, 1): (small(0), chunk(0, 2), state(0), small(1)),
    (BACKWARD_DONE, 0, 0, 1): (small(0), chunk(0, 2)),
}
LAST = ()


def whole_kernel(names, *refs):
    r = SimpleNamespace(**dict(zip(names, refs)))
    program = Program(r)
    place = program.place
    barrier = greet(
        [place.along_seq(k) for k in range(1, SEQ)] + [place.along_head(k) for k in range(1, HEAD)]
    )
    program.start_loads()
    r.small[...] = jnp.zeros_like(r.small)
    r.misc[...] = jnp.zeros_like(r.misc)
    pl.semaphore_wait(barrier, SEQ - 1 + HEAD - 1)
    tasks = {}

    def go_on(task):
        if task not in tasks:
            tasks[task] = task[0](program, *task[1:])
        if next(tasks[task], StopIteration) is StopIteration:
            tasks[task] = iter(())

    live = {b: chain(program, b) for b in range(SEQS)}
    turn = 0
    while live:
        turn += 1
        for b in list(live):
            if turn <= LAG * b:
                continue
            at = next(live[b], None)
            if at is None:
                del live[b]
                continue
            for name in BEHIND.get((*at, b), ()):
                go_on(name)
    program.put(r.grad.at[0], r.hidden_grad)
    for task in LAST:
        go_on(task)
    for task in list(tasks) * 8:
        go_on(task)
    for copy in program.stores:
        copy.wait()
    program.mail.finish()


def floats(*shape):
    return pltpu.VMEM(shape, F32)


def lows(*shape):
    return pltpu.VMEM(shape, LOW)


def dma(*shape):
    return pltpu.SemaphoreType.DMA(shape)


def run(args):
    inputs = dict(
        hidden_in=pl.ANY,
        cotangent_in=pl.ANY,
        norm_gain=pltpu.VMEM,
        inner_in=pl.ANY,
        state_in=pl.ANY,
        step=pltpu.VMEM,
        conv_weight=pltpu.VMEM,
        conv_bias=pltpu.VMEM,
        conv_state_weight=pltpu.VMEM,
        conv_state_bias=pltpu.VMEM,
        step_bias=pltpu.VMEM,
        decay_log=pltpu.VMEM,
        skip_gain=pltpu.VMEM,
        mixer_gain=pltpu.VMEM,
        output_in=pl.ANY,
    )
    outputs = dict(
        hidden_out=((SEQS, LOCAL, WIDTH), pl.ANY),
        hidden_grad=((SEQS, LOCAL, WIDTH), pl.ANY),
        pair_grad=((LAYERS, 2, BLOCK, INNER), pltpu.VMEM),
        state_grad=((LAYERS, HEAD, PART, LANES), pltpu.VMEM),
        step_grad=((LAYERS, 8, LANES), pltpu.VMEM),
        small_out=((LAYERS, SEQ, SMALL_PIECE, LANES), pltpu.VMEM),
        output_grad=((LAYERS, BLOCK, INNER), pltpu.VMEM),
    )
    flows = 2 * CHUNKS
    copies = (
        (2 * LAYERS + 2 * LAYERS) * HEAD_SUM_COPIES
        + LAYERS * SEQS * (2 + HEAD - 1)
        + 3 * LAYERS * (HEAD - 1)
        + LAYERS * flows * 12
    )
    scratch = dict(
        res=floats(LAYERS + 1, ROWS, WIDTH),
        grad=floats(LAYERS + 1, ROWS, WIDTH),
        inner=lows(LAYERS, 2, WIDTH, INNER),
        state=lows(LAYERS, WIDTH, 2 * STATE),
        wout=lows(LAYERS, WIDTH, INNER),
        normed=lows(LAYERS, ROWS, WIDTH),
        gate=floats(LAYERS, ROWS, INNER),
        raw=floats(LAYERS, SEQS, 8 + LOCAL, CONV),
        pre=floats(LAYERS, ROWS, CONV),
        act=lows(LAYERS, ROWS, CONV),
        dt=floats(LAYERS, ROWS, LANES),
        logs=floats(LAYERS, ROWS, LANES),
        sig=floats(LAYERS, ROWS, LANES),
        y=floats(LAYERS, ROWS, INNER),
        s0=floats(LAYERS, SEQS * INNER, STATE),
        factor=floats(LAYERS, ROWS, LANES),
        means=floats(ROWS, LANES),
        dmixed=floats(ROWS, INNER),
        gated=floats(ROWS, INNER),
        sums=floats(LAYERS, SEQS, 8, LOCAL),
        sums_seen=floats(LAYERS, SEQS, HEAD, 8, LOCAL),
        halo=floats(LAYERS, SEQS, 8, WIDTH),
        part=floats(ROWS, WIDTH),
        pair=floats(SEQS, HALVED, WIDTH),
        half_p=floats(SEQS, SHARE // 2, WIDTH),
        half_n=floats(SEQS, SHARE // 2, WIDTH),
        near_p=floats(SEQS, SHARE, WIDTH),
        near_n=floats(SEQS, SHARE, WIDTH),
        last_part=floats(ROWS, WIDTH),
        last_pair=floats(SEQS, HALVED, WIDTH),
        last_half_p=floats(SEQS, SHARE // 2, WIDTH),
        last_half_n=floats(SEQS, SHARE // 2, WIDTH),
        last_near_p=floats(SEQS, SHARE, WIDTH),
        last_near_n=floats(SEQS, SHARE, WIDTH),
        state_part=floats(LAYERS, 2 * STATE, ROWS),
        state_seen=floats(LAYERS, HEAD, PART, ROWS),
        stage=floats(SEQ, PIECE + 8, LANES),
        seen=floats(SEQ, PIECE + 8, LANES),
        turned=floats(SEQ, PIECE, LANES),
        back=floats(SEQ, PIECE, LANES),
        grad_low=lows(LAYERS, ROWS, WIDTH),
        mixed=lows(LAYERS, ROWS, INNER),
        dproj=lows(LAYERS, ROWS, PROJ),
        dy=floats(ROWS, INNER),
        dact=floats(ROWS, CONV),
        dlogs=floats(SEQS, 2, LOCAL, LANES),
        dpre=floats(SEQS, LOCAL + 8, CONV),
        edge=floats(LAYERS, SEQS, 8, CONV),
        edge_seen=floats(LAYERS, SEQS, 8, CONV),
        small=floats(LAYERS, SMALL, LANES),
        own=floats(CHUNKS, RING, RING, BLOCK, INNER),
        a1p=floats(flows, RING, QUARTER, INNER),
        a1n=floats(flows, RING, QUARTER, INNER),
        a2p=floats(flows, RING, HALF, INNER),
        a2n=floats(flows, RING, HALF, INNER),
        asum=floats(flows, RING, HALF, INNER),
        a3p=floats(flows, QUARTER, INNER),
        a3n=floats(flows, QUARTER, INNER),
        a4p=floats(flows, HALF, INNER),
        a4n=floats(flows, HALF, INNER),
        misc=floats(LAYERS, SEQ, MISC, LANES),
        misc_seen=floats(LAYERS, SEQ, MISC, LANES),
        shared=floats(LAYERS, PART, LANES),
        shared_seen=floats(LAYERS, HEAD, PART, LANES),
        tiny=floats(LAYERS, SMALL_PIECE, LANES),
        tiny_seen=floats(LAYERS, SEQ, SMALL_PIECE, LANES),
        tiny_heads=floats(LAYERS, HEAD, SMALL_PIECE, LANES),
        small_seen=floats(LAYERS, SEQ, SMALL_PIECE, LANES),
        mail_send=dma(copies),
        mail_recv=dma(copies),
        leg1_send=dma(SEQ),
        leg1_recv=dma(SEQ),
        leg2_send=dma(SEQ),
        leg2_recv=dma(SEQ),
        scatter_send=dma(LAYERS, SEQ),
        scatter_recv=dma(LAYERS, SEQ),
        tiny_send=dma(LAYERS, SEQ),
        tiny_recv=dma(LAYERS, SEQ),
        gather_send=dma(LAYERS, SEQ),
        gather_recv=dma(LAYERS, SEQ),
        load=dma(2 * SEQS + 4 * LAYERS),
        store=dma(2 * SEQS),
    )
    results = pl.pallas_call(
        partial(whole_kernel, list(inputs) + list(outputs) + list(scratch)),
        out_shape=[jax.ShapeDtypeStruct(shape, F32) for shape, _ in outputs.values()],
        in_specs=[pl.BlockSpec(memory_space=space) for space in inputs.values()],
        out_specs=[pl.BlockSpec(memory_space=space) for _, space in outputs.values()],
        scratch_shapes=list(scratch.values()),
        compiler_params=pltpu.CompilerParams(
            collective_id=0, has_side_effects=True, vmem_limit_bytes=VMEM_LIMIT
        ),
    )(*args)
    return SimpleNamespace(**dict(zip(outputs, results)))


def pack_kernel(
    whole_out,
    whole_grad,
    pair_in,
    state_in,
    step_in,
    small,
    output_in,
    hidden_out,
    hidden_grad,
    norm_gain,
    pair,
    state,
    step,
    conv_weight,
    conv_bias,
    conv_state_weight,
    conv_state_bias,
    step_bias,
    decay_log,
    skip_gain,
    mixer_gain,
    output,
):
    hidden_out[...] = whole_out[...]
    hidden_grad[...] = whole_grad[...]
    output[...] = output_in[...]

    def lanes(l, first, count):
        rows = [small[l, (first + k) // 8, (first + k) % 8 : (first + k) % 8 + 1, :] for k in range(count)]
        return jnp.concatenate(rows, axis=1)

    for l in range(LAYERS):
        one = slice(l, l + 1)
        for part in range(2):
            pair[l, :, part, :] = pair_in[l, part]
        columns = state_in[l].reshape(2 * STATE, LANES)
        for half in range(2):
            cols = slice(half * STATE, (half + 1) * STATE)
            state[l, :, cols] = columns[cols].T[:BLOCK]
        norm_gain[one, :] = lanes(l, 33, 12)
        wide = jnp.concatenate([step_in[l], jnp.zeros((LANES - 8, LANES), F32)], axis=0).T
        step[l] = wide[:BLOCK, :HEADS]
        for tap in range(4):
            conv_weight[l, tap : tap + 1, :] = lanes(l, 13 + 5 * tap, 3)
            conv_state_weight[l, tap : tap + 1, :] = lanes(l, 16 + 5 * tap, 2)
        conv_bias[one, :] = lanes(l, 8, 3)
        conv_state_bias[one, :] = lanes(l, 11, 2)
        step_bias[one, :] = lanes(l, 6, 1)[:, :HEADS]
        decay_log[one, :] = lanes(l, 7, 1)[:, :HEADS]
        skip = dot_nt(jnp.broadcast_to(lanes(l, 3, 3), (8, INNER)), head_lanes(), HIGHEST)
        skip_gain[one, :] = skip[0:1, :HEADS]
        mixer_gain[one, :] = lanes(l, 0, 3)


def shards(*args):
    args = list(args)
    args[3] = args[3].transpose(0, 2, 1, 3)
    args[5] = args[5].transpose(0, 2, 1)
    out = run(args)
    big = (SEQS, LOCAL, WIDTH)
    shapes = [
        big,
        big,
        (LAYERS, WIDTH),
        (LAYERS, BLOCK, 2, INNER),
        (LAYERS, BLOCK, 2 * STATE),
        (LAYERS, BLOCK, HEADS),
        (LAYERS, 4, INNER),
        (LAYERS, INNER),
        (LAYERS, 4, 2 * STATE),
        (LAYERS, 2 * STATE),
        (LAYERS, HEADS),
        (LAYERS, HEADS),
        (LAYERS, HEADS),
        (LAYERS, INNER),
        (LAYERS, BLOCK, INNER),
    ]
    held = [pl.BlockSpec(memory_space=pltpu.VMEM)]
    return tuple(
        pl.pallas_call(
            pack_kernel,
            out_shape=[jax.ShapeDtypeStruct(shape, F32) for shape in shapes],
            in_specs=held * 7,
            out_specs=held * 15,
        )(
            out.hidden_out,
            out.hidden_grad,
            out.pair_grad,
            out.state_grad,
            out.step_grad,
            out.small_out,
            out.output_grad,
        )
    )


def solution(mesh):
    heads = P(None, None, "head")
    in_specs = (
        P(None, "seq", None),
        P(None, "seq", None),
        P(),
        P(None, None, None, "head"),
        P(),
        heads,
        heads,
        P(None, "head"),
        P(),
        P(),
        P(None, "head"),
        P(None, "head"),
        P(None, "head"),
        P(None, "head"),
        heads,
    )
    out_specs = (
        P(None, "seq", None),
        P(None, "seq", None),
        P(),
        P(None, "seq", None, "head"),
        P(None, "seq", None),
        P(None, "seq", "head"),
        heads,
        P(None, "head"),
        P(),
        P(),
        P(None, "head"),
        P(None, "head"),
        P(None, "head"),
        P(None, "head"),
        P(None, "seq", "head"),
    )
    return jax.shard_map(shards, mesh=mesh, in_specs=in_specs, out_specs=out_specs, check_vma=False)
```

```python
from types import SimpleNamespace

from functools import partial

import jax
import jax.numpy as jnp
from jax import lax
from jax.experimental import pallas as pl
from jax.experimental.pallas import tpu as pltpu
from jax.sharding import PartitionSpec as P

MESH = pl.DeviceIdType.MESH
HIGHEST = lax.Precision.HIGHEST
EPSILON = 1e-05
F32 = jnp.float32
LOW = jnp.bfloat16

RING = 4
SEQ = 16
HEAD = 8
SEQS = 2
LOCAL = 128
ROWS = SEQS * LOCAL
WIDTH = 1536
INNER = 384
TOTAL = 3072
HEADS = 6
STATE = 128
CONV = INNER + 2 * STATE
PROJ = 2 * INNER + 2 * STATE + 128
LANES = 128
PIECE = SEQS * INNER // SEQ
OWNERS = SEQ // SEQS
GROUPS = PIECE // 16
LAYERS = 2
HALVED = LOCAL // 2
SHARE = LOCAL // HEAD
BLOCK = WIDTH // SEQ
VMEM_LIMIT = 62 * 1024 * 1024


def dot(a, b, precision=None):
    return lax.dot_general(a, b, (((1,), (0,)), ((), ())), precision=precision, preferred_element_type=F32)


def dot_nt(a, b, precision=None):
    return lax.dot_general(a, b, (((1,), (1,)), ((), ())), precision=precision, preferred_element_type=F32)


def dot_tn(a, b, precision=None):
    return lax.dot_general(a, b, (((0,), (0,)), ((), ())), precision=precision, preferred_element_type=F32)


class Place:
    def __init__(self):
        self.s = lax.axis_index("seq")
        self.h = lax.axis_index("head")
        self.x, self.y = lax.rem(self.s, RING), lax.div(self.s, RING)
        self.core, self.z = lax.rem(self.h, 2), lax.div(self.h, 2)

    def seq(self, steps):
        return lax.rem(self.s + steps + SEQ, SEQ)

    def along_seq(self, steps):
        return (self.seq(steps), self.h)

    def along_head(self, steps):
        return (self.s, lax.rem(self.h + steps, HEAD))

    def partner(self):
        return (self.s, self.h + 1 - 2 * self.core)

    def x_at(self, steps):
        return lax.rem(self.x + steps + RING, RING)

    def y_at(self, steps):
        return lax.rem(self.y + steps + RING, RING)

    def z_at(self, steps):
        return lax.rem(self.z + steps + RING, RING)

    def along_x(self, steps):
        return (self.y * RING + self.x_at(steps), self.h)

    def along_y(self, steps):
        return (self.y_at(steps) * RING + self.x, self.h)

    def along_z(self, steps):
        return (self.s, self.z_at(steps) * 2 + self.core)


class Message:
    def __init__(self, copy):
        self.copy, self.out = copy, True

    def wait_recv(self):
        self.copy.wait_recv()

    def done(self):
        if self.out:
            self.copy.wait_send()
            self.out = False


class Mail:
    def __init__(self, send, recv):
        self.send, self.recv, self.sent = send, recv, []

    def copy(self, src, dst, to):
        at = len(self.sent)
        copy = pltpu.make_async_remote_copy(
            src_ref=src,
            dst_ref=dst,
            send_sem=self.send.at[at],
            recv_sem=self.recv.at[at],
            device_id=to,
            device_id_type=MESH,
        )
        copy.start()
        self.sent.append(Message(copy))
        return self.sent[-1]

    def finish(self):
        for message in self.sent:
            message.done()


def greet(peers):
    barrier = pltpu.get_barrier_semaphore()
    for peer in peers:
        pl.semaphore_signal(barrier, inc=1, device_id=peer, device_id_type=MESH)
    return barrier


def masks():
    row = lax.broadcasted_iota(jnp.int32, (LOCAL, LOCAL), 0)
    column = lax.broadcasted_iota(jnp.int32, (LOCAL, LOCAL), 1)
    return row, column


def head_lanes():
    head = lax.broadcasted_iota(jnp.int32, (LANES, INNER), 0)
    channel = lax.broadcasted_iota(jnp.int32, (LANES, INNER), 1)
    return (lax.div(channel, INNER // HEADS) == head).astype(F32)


def split_pair(pair):
    first = lax.broadcasted_iota(jnp.int32, (LOCAL, LANES), 1) < LANES // 2
    zero = jnp.zeros_like(pair)
    return jnp.concatenate([jnp.where(first, pair, zero), jnp.where(first, zero, pair)], axis=0)


def two(values, axis):
    high = values.astype(LOW)
    return jnp.concatenate([high, (values - high.astype(F32)).astype(LOW)], axis=axis)


def twice(values, axis):
    return jnp.concatenate([values, values], axis=axis)


def product_of_two(a, b):
    high, low = b[:, :STATE], b[:, STATE:]
    return dot(a, twice(high, 0)) + dot(a[:, :INNER], low)


def rms_factor(rows):
    return lax.rsqrt(jnp.mean(rows * rows, axis=-1, keepdims=True) + EPSILON)


def head_row(ref, layer):
    return jnp.concatenate([ref[layer : layer + 1, :], jnp.zeros((1, LANES - HEADS), F32)], axis=1)


def row(ref, layer):
    return ref[layer : layer + 1, :]


def seq_rows(at):
    return slice(at * LOCAL, (at + 1) * LOCAL)


def head_sum(place, mail, part, pair, half_p, half_n, near_p, near_n, whole, first_row, finalize):
    core, z = place.core, place.z
    half = SHARE // 2

    def rows(of_core, of_z, first=0, count=SHARE):
        return pl.ds(pl.multiple_of(first_row + of_core * HALVED + of_z * SHARE + first, 8), count)

    def pair_rows(of_z):
        return pl.ds(pl.multiple_of(of_z * SHARE, 8), SHARE)

    partner, above_to, below_to = place.partner(), place.along_z(1), place.along_z(-1)
    posted = []

    def post(src, dst, to):
        posted.append(mail.copy(src, dst, to))
        return posted[-1]

    swapped = {}
    for step in (2, 1, 3, 0):
        at = place.z_at(step)
        swapped[step] = post(part.at[rows(1 - core, at)], pair.at[pair_rows(at)], partner)
    yield

    def join(step):
        at = place.z_at(step)
        swapped[step].wait_recv()
        part[rows(core, at), :] += pair[pair_rows(at), :]

    join(2)
    far, above, below = place.z_at(2), place.z_at(1), place.z_at(-1)
    first, last = pl.ds(0, half), pl.ds(half, half)
    up = post(part.at[rows(core, far, 0, half)], half_p, above_to)
    down = post(part.at[rows(core, far, half, half)], half_n, below_to)
    join(1)
    near = [post(part.at[rows(core, above, half, half)], near_p.at[last], above_to)]
    join(3)
    near.append(post(part.at[rows(core, below, 0, half)], near_n.at[first], below_to))
    join(0)
    yield
    up.wait_recv()
    part[rows(core, above, 0, half), :] += half_p[...]
    near.append(post(part.at[rows(core, above, 0, half)], near_p.at[first], above_to))
    down.wait_recv()
    part[rows(core, below, half, half), :] += half_n[...]
    near.append(post(part.at[rows(core, below, half, half)], near_n.at[last], below_to))
    yield
    for message in near:
        message.wait_recv()
    mine = rows(core, z)
    whole[mine, :] = finalize(part[mine, :] + near_p[...] + near_n[...], mine)
    up = post(whole.at[mine], whole.at[mine], above_to)
    down = post(whole.at[mine], whole.at[mine], below_to)
    across = [post(whole.at[mine], whole.at[mine], partner)]
    yield
    up.wait_recv()
    piece = rows(core, below, 0, half)
    up = post(whole.at[piece], whole.at[piece], above_to)
    piece = rows(core, below)
    across.append(post(whole.at[piece], whole.at[piece], partner))
    down.wait_recv()
    piece = rows(core, above, half, half)
    down = post(whole.at[piece], whole.at[piece], below_to)
    piece = rows(core, above)
    across.append(post(whole.at[piece], whole.at[piece], partner))
    yield
    up.wait_recv()
    piece = rows(core, far, 0, half)
    across.append(post(whole.at[piece], whole.at[piece], partner))
    down.wait_recv()
    piece = rows(core, far, half, half)
    across.append(post(whole.at[piece], whole.at[piece], partner))
    yield
    for message in across:
        message.wait_recv()
    for message in posted:
        message.done()


HEAD_SUM_COPIES = 4 + 2 + 4 + 2 + 2 + 5


class Exchange:
    def __init__(self, place, r, l, at, reverse):
        self.place, self.r, self.l, self.at, self.reverse = place, r, l, at, reverse
        self.rows = pl.ds(0, PIECE if reverse else PIECE + 8)
        self.owner = lax.rem(place.x + place.y, SEQS) == at
        self.owners = [RING * y + x for y in range(RING) for x in range(RING) if (x + y) % SEQS == at]

    def to_owner(self, k):
        owner = self.owners[k]
        r, s = self.r, self.place.s
        return pltpu.make_async_remote_copy(
            src_ref=r.stage.at[owner, self.rows],
            dst_ref=r.seen.at[s, self.rows],
            send_sem=r.leg1_send.at[owner],
            recv_sem=r.leg1_recv.at[s],
            device_id=(owner, self.place.h),
            device_id_type=MESH,
        )

    def from_source(self, k):
        r, source = self.r, self.place.seq(k)
        return pltpu.make_async_remote_copy(
            src_ref=r.stage.at[source, self.rows],
            dst_ref=r.seen.at[source, self.rows],
            send_sem=r.leg1_send.at[source],
            recv_sem=r.leg1_recv.at[source],
            device_id=(source, self.place.h),
            device_id_type=MESH,
        )

    def to_device(self, k):
        r, s, to = self.r, self.place.s, self.place.seq(k)
        return pltpu.make_async_remote_copy(
            src_ref=r.turned.at[to],
            dst_ref=r.back.at[s],
            send_sem=r.leg2_send.at[to],
            recv_sem=r.leg2_recv.at[s],
            device_id=(to, self.place.h),
            device_id_type=MESH,
        )

    def from_owner(self, k):
        owner = self.owners[k]
        r = self.r
        return pltpu.make_async_remote_copy(
            src_ref=r.turned.at[owner],
            dst_ref=r.back.at[owner],
            send_sem=r.leg2_send.at[owner],
            recv_sem=r.leg2_recv.at[owner],
            device_id=(owner, self.place.h),
            device_id_type=MESH,
        )

    def each_owner(self, what):
        for k in range(OWNERS):

            @pl.when(self.owners[k] != self.place.s)
            def _(k=k):
                what(k)

    def start(self, state, decays=None):
        r = self.r
        for piece in range(OWNERS):
            slot = self.owners[piece]
            r.stage[slot, 0:PIECE, :] = state[piece * PIECE : (piece + 1) * PIECE]
            if self.reverse:
                continue
            for group in range(GROUPS):
                head = (piece * GROUPS + group) // 4
                r.stage[slot, PIECE + group : PIECE + group + 1, :] = decays[head]
            r.stage[slot, PIECE + GROUPS : PIECE + 8, :] = jnp.zeros((8 - GROUPS, LANES), F32)
        self.each_owner(lambda k: self.to_owner(k).start())

        @pl.when(self.owner)
        def _():
            r.seen[self.place.s] = r.stage[self.place.s]

    def turn(self):
        r = self.r

        @pl.when(self.owner)
        def _():
            def landed(k, carry):
                self.from_source(k).wait_recv()
                return carry

            lax.fori_loop(1, SEQ, landed, 0)
            if not self.reverse:
                r.kept[self.l] = r.seen[:, PIECE:, :]

            def hop(step, carry):
                at = SEQ - 1 - step if self.reverse else step
                for group in range(GROUPS):
                    r.turned[at, group * 16 : group * 16 + 16, :] = carry[group]
                return tuple(
                    r.kept[self.l, at, group : group + 1, :] * carry[group]
                    + r.seen[at, group * 16 : group * 16 + 16, :]
                    for group in range(GROUPS)
                )

            lax.fori_loop(0, SEQ, hop, tuple(jnp.zeros((16, LANES), F32) for _ in range(GROUPS)))

            def send(k, carry):
                self.to_device(k).start()
                return carry

            lax.fori_loop(1, SEQ, send, 0)
            r.back[self.place.s] = r.turned[self.place.s]

    def finish(self):
        self.each_owner(lambda k: self.from_owner(k).wait_recv())
        self.each_owner(lambda k: self.to_owner(k).wait_send())

        @pl.when(self.owner)
        def _():
            def left(k, carry):
                self.to_device(k).wait_send()
                return carry

            lax.fori_loop(1, SEQ, left, 0)

        return jnp.concatenate([self.r.back[owner] for owner in self.owners], axis=0)


SMALL = 128
SMALL_PIECE = SMALL // SEQ
PART = 2 * STATE // HEAD
MISC = PART + 8
SHARED = ((11, 13), (16, 18), (21, 23), (26, 28), (31, 33), (33, 45))
HALF = BLOCK // 2
QUARTER = BLOCK // 4
CHUNKS = 3


class Program:
    def __init__(self, r):
        self.r = r
        self.place = Place()
        self.mail = Mail(r.mail_send, r.mail_recv)
        self.loads = {}
        self.sums_sent = {}
        self.stores = []


    def load(self, name, src, dst):
        copy = pltpu.make_async_copy(src, dst, self.r.load.at[len(self.loads)])
        copy.start()
        self.loads[name] = copy

    def need(self, *names):
        for name in names:
            copy = self.loads.get(name)
            if copy is not None:
                copy.wait()
                self.loads[name] = None

    def load_weights(self, l):
        r = self.r
        self.load((1, l), r.inner_in.at[l, 1], r.inner.at[l, 1])
        self.load((2, l), r.state_in.at[l], r.state.at[l])
        self.load((3, l), r.inner_in.at[l, 0], r.inner.at[l, 0])
        self.load((4, l), r.output_in.at[l], r.wout.at[l])

    def start_loads(self):
        r = self.r
        for b in range(SEQS):
            self.load((0, b), r.hidden_in.at[b], r.res.at[0, pl.ds(b * LOCAL, LOCAL)])
        self.load_weights(0)

    def more_loads(self):
        r = self.r
        for l in range(1, LAYERS):
            self.load_weights(l)
        for b in range(SEQS):
            self.load((5, b), r.cotangent_in.at[b], r.grad.at[LAYERS, pl.ds(b * LOCAL, LOCAL)])

    def put(self, source, target):
        for b in range(SEQS):
            copy = pltpu.make_async_copy(
                source.at[pl.ds(b * LOCAL, LOCAL)], target.at[b], self.r.store.at[len(self.stores)]
            )
            copy.start()
            self.stores.append(copy)

    def store(self):
        self.put(self.r.res.at[LAYERS], self.r.hidden_out)
        yield

    def head_summing(self, l, b, part, extra, whole, finalize):
        r = self.r
        pair, half_p, half_n, near_p, near_n = extra
        return head_sum(
            self.place,
            self.mail,
            part,
            pair.at[b],
            half_p.at[b],
            half_n.at[b],
            near_p.at[b],
            near_n.at[b],
            whole,
            b * LOCAL,
            finalize,
        )

    def wide(self):
        r = self.r
        return r.pair, r.half_p, r.half_n, r.near_p, r.near_n

    def last(self):
        r = self.r
        return r.last_pair, r.last_half_p, r.last_half_n, r.last_near_p, r.last_near_n

    def add_small(self, l, at, values):
        for k in range(values.shape[1] // LANES):
            self.r.small[l, at + k : at + k + 1, :] += values[:, k * LANES : (k + 1) * LANES]

    def taps(self, l, tap):
        r = self.r
        return jnp.concatenate([r.conv_weight[l, tap : tap + 1, :], r.conv_state_weight[l, tap : tap + 1, :]], axis=1)

    def decays(self, l, b):
        r = self.r
        decay = jnp.exp(r.logs[l, (b + 1) * LOCAL - 1 : (b + 1) * LOCAL, :])
        return [jnp.broadcast_to(decay[:, h : h + 1], (1, LANES)) for h in range(HEADS)]

    def pass_on(self, l, b):
        rows = self.r.res.at[l, pl.ds((b + 1) * LOCAL - 8, 8)]
        return self.mail.copy(rows, self.r.halo.at[l, b], self.place.along_seq(1))

    def forward(self, l, b):
        r, place, mail = self.r, self.place, self.mail
        here = seq_rows(b)
        gain = row(r.norm_gain, l)
        self.need((0, b))

        def norm_rows(at, carry):
            rows = pl.ds(pl.multiple_of(b * LOCAL + at * 32, 32), 32)
            values = r.res[l, rows, :]
            r.normed[l, rows, :] = (values * rms_factor(values) * gain).astype(LOW)
            return carry

        if l > 0:
            edge = self.pass_on(l, b)
        lax.fori_loop(0, LOCAL // 32, norm_rows, 0)
        self.need((1, l), (2, l))
        normed = r.normed[l, here, :]
        r.raw[l, b, 8:, :INNER] = dot(normed, r.inner[l, 1])
        r.raw[l, b, 8:, INNER:] = dot(normed, r.state[l])
        if l == 0:
            if b == 0:
                pl.semaphore_wait(self.barrier, SEQ - 1 + HEAD - 1)
            edge = self.pass_on(l, b)
        pushed = jnp.concatenate([dot_nt(normed, r.step[l]), jnp.zeros((LOCAL, LANES - HEADS), F32)], axis=1)
        pushed = pushed + head_row(r.step_bias, l)
        sizes = jax.nn.softplus(pushed)
        r.dt[l, here, :] = sizes
        r.sig[l, here, :] = jax.nn.sigmoid(pushed)
        rows, columns = masks()
        lower = (rows >= columns).astype(F32)
        rate = -jnp.exp(head_row(r.decay_log, l))
        r.logs[l, here, :] = dot(lower, sizes * rate, HIGHEST)
        yield
        edge.wait_recv()
        values = r.halo[l, b]
        borrowed = jnp.where(place.s == 0, 0.0, values * rms_factor(values) * gain).astype(LOW)
        r.raw[l, b, 0:8, :INNER] = dot(borrowed, r.inner[l, 1])
        r.raw[l, b, 0:8, INNER:] = dot(borrowed, r.state[l])
        summed = jnp.concatenate([row(r.conv_bias, l), row(r.conv_state_bias, l)], axis=1)
        for tap in range(4):
            summed = summed + self.taps(l, tap) * r.raw[l, b, 5 + tap : 5 + tap + LOCAL, :]
        r.pre[l, here, :] = summed
        r.act[l, here, :] = (summed * jax.nn.sigmoid(summed)).astype(LOW)
        lanes = head_lanes()
        ending = r.logs[l, (b + 1) * LOCAL - 1 : (b + 1) * LOCAL, :]
        tail = dot(jnp.exp(ending - r.logs[l, here, :]) * r.dt[l, here, :], lanes, HIGHEST)
        xs, bs, cs = r.act[l, here, :INNER], r.act[l, here, INNER : INNER + STATE], r.act[l, here, INNER + STATE :]
        exchange = Exchange(place, r, l, b, False)
        exchange.start(dot_tn(two(xs.astype(F32) * tail, 0), twice(bs, 0)), self.decays(l, b))
        yield
        if (l, b) == (0, 0):
            self.more_loads()
        self.need((3, l))
        r.gate[l, here, :] = dot(normed, r.inner[l, 0])
        scores = jnp.where(rows >= columns, dot_nt(cs, bs), 0.0)
        turned_logs = r.logs[l, here, :].T
        turned_dt = r.dt[l, here, :].T
        for p in range(HEADS // 2):
            weights = []
            for h in (2 * p, 2 * p + 1):
                fall = jnp.minimum(r.logs[l, here, h : h + 1] - turned_logs[h : h + 1, :], 0.0)
                weights.append(scores * jnp.exp(fall) * turned_dt[h : h + 1, :])
            cols = slice(p * LANES, (p + 1) * LANES)
            r.y[l, here, cols] = dot(two(jnp.concatenate(weights, axis=1), 1), twice(split_pair(xs[:, cols]), 0))
        yield
        exchange.turn()
        yield
        start = exchange.finish()
        r.s0[l, b * INNER : (b + 1) * INNER, :] = start
        grown = dot(jnp.exp(r.logs[l, here, :]), lanes, HIGHEST)
        skip = dot(head_row(r.skip_gain, l), lanes, HIGHEST)
        values = r.y[l, here, :] + dot_nt(twice(cs, 1), two(start, 1)) * grown + skip * xs.astype(F32)
        r.y[l, here, :] = values
        gates = r.gate[l, here, :]
        gated = values * (gates * jax.nn.sigmoid(gates))
        ones = jnp.ones((8, INNER), F32)
        sums = dot_nt(ones, gated * gated, HIGHEST)
        mixer = row(r.mixer_gain, l)
        self.need((4, l))
        if l == LAYERS - 1:
            self.need((5, b))
            r.grad_low[l, here, :] = r.grad[LAYERS, here, :].astype(LOW)
            dmixed = dot(r.grad_low[l, here, :], r.wout[l])
            r.dmixed[here, :] = dmixed
            inner_sums = dot_nt(ones, dmixed * mixer * gated, HIGHEST)
            first = lax.broadcasted_iota(jnp.int32, (8, LOCAL), 0) == 0
            sums = jnp.where(first, sums, inner_sums)
        r.sums[l, b] = sums
        r.sums_seen[l, b, place.h] = sums
        self.sums_sent[l, b] = [
            mail.copy(r.sums.at[l, b], r.sums_seen.at[l, b, place.h], place.along_head(k)) for k in range(1, HEAD)
        ]
        r.gated[here, :] = gated
        yield
        self.over_head(l, b)
        r.mixed[l, here, :] = (r.gated[here, :] * r.factor[l, here, :][:, :1] * mixer).astype(LOW)
        part = r.part if l < LAYERS - 1 else r.last_part
        part[here, :] = dot_nt(r.mixed[l, here, :], r.wout[l])

    def over_head(self, l, b):
        r = self.r
        for message in self.sums_sent[l, b]:
            message.wait_recv()
        sums = r.sums_seen[l, b, 0]
        for k in range(1, HEAD):
            sums = sums + r.sums_seen[l, b, k]
        columns = jnp.concatenate([sums, jnp.zeros((LOCAL - 8, LOCAL), F32)], axis=0).T
        factor = lax.rsqrt(columns[:, 0:1] / TOTAL + EPSILON)
        r.factor[l, seq_rows(b), :] = jnp.broadcast_to(factor, (LOCAL, LANES))
        r.means[seq_rows(b), :] = jnp.broadcast_to(columns[:, 1:2] * factor / TOTAL, (LOCAL, LANES))

    def forward_sum(self, l, b):
        r = self.r

        def finalize(total, mine):
            return r.res[l, mine, :] + total

        if l < LAYERS - 1:
            return self.head_summing(l, b, r.part, self.wide(), r.res.at[l + 1], finalize)
        return self.head_summing(l, b, r.last_part, self.last(), r.res.at[l + 1], finalize)

    def backward(self, l, b):
        r, place, mail = self.r, self.place, self.mail
        here = seq_rows(b)
        lanes = head_lanes()
        rows, columns = masks()
        mixer = row(r.mixer_gain, l)
        skip = dot(head_row(r.skip_gain, l), lanes, HIGHEST)
        xs, bs, cs = r.act[l, here, :INNER], r.act[l, here, INNER : INNER + STATE], r.act[l, here, INNER + STATE :]
        if l == LAYERS - 1:
            dmixed, means = r.dmixed[here, :], r.means[here, :][:, :1]
        else:
            low = r.grad[l + 1, here, :].astype(LOW)
            r.grad_low[l, here, :] = low
            dmixed = dot(low, r.wout[l])
            branch = r.res[l + 1, here, :] - r.res[l, here, :]
            means = jnp.sum(low.astype(F32) * branch, axis=-1, keepdims=True) / TOTAL
        factor = r.factor[l, here, :][:, :1]
        gates, values = r.gate[l, here, :], r.y[l, here, :]
        opened = jax.nn.sigmoid(gates)
        silu = gates * opened
        q = values * silu * factor
        self.add_small(l, 0, jnp.sum(dmixed * q, axis=0, keepdims=True))
        dgated = factor * (dmixed * mixer - q * means)
        dvalues = dgated * silu
        r.dy[here, :] = dvalues
        r.dproj[l, here, :INNER] = (dgated * values * opened * (1.0 + gates * (1.0 - opened))).astype(LOW)
        self.add_small(l, 3, jnp.sum(dvalues * xs.astype(F32), axis=0, keepdims=True))
        grown = dot(jnp.exp(r.logs[l, here, :]), lanes, HIGHEST)
        scaled = two(grown * dvalues, 1)
        exchange = Exchange(place, r, l, b, True)
        exchange.start(dot_tn(two(grown * dvalues, 0), twice(cs, 0)))
        yield
        inside = (rows >= columns).astype(F32)
        scores = dot_nt(cs, bs) * inside
        turned_logs = r.logs[l, here, :].T
        turned_dt = r.dt[l, here, :].T
        dscores = jnp.zeros((LOCAL, LOCAL), F32)
        row_sums, column_sums = [], []
        for p in range(HEADS // 2):
            cols = slice(p * LANES, (p + 1) * LANES)
            dys = two(split_pair(r.dy[here, cols]), 1)
            both = dot_nt(dys, twice(xs[:, cols], 1))
            weights = []
            for k in range(2):
                h = 2 * p + k
                fall = jnp.exp(jnp.minimum(r.logs[l, here, h : h + 1] - turned_logs[h : h + 1, :], 0.0))
                steps = turned_dt[h : h + 1, :]
                weights.append(scores * fall * steps)
                moved = both[k * LOCAL : (k + 1) * LOCAL] * fall
                dscores += moved * steps
                moved = moved * scores
                column_sums.append(jnp.sum(moved, axis=0, keepdims=True))
                row_sums.append(jnp.sum(moved * steps, axis=1, keepdims=True))
            weights = two(jnp.concatenate(weights, axis=0), 0)
            high, low = dys[:, :LANES], dys[:, LANES:]
            r.dact[here, cols] = dot_tn(weights, twice(high, 0)) + dot_tn(weights[:SEQS * LOCAL], low)
        dscores = dscores * inside
        start = two(r.s0[l, b * INNER : (b + 1) * INNER, :], 1)
        r.dact[here, INNER : INNER + STATE] = dot_tn(two(dscores, 0), twice(cs, 0))
        r.dact[here, INNER + STATE :] = dot(two(dscores, 1), twice(bs, 0)) + product_of_two(scaled, start)
        carried = dot_nt(twice(cs, 1), start)
        from_start = dot_nt(carried * r.dy[here, :], lanes, HIGHEST) * jnp.exp(r.logs[l, here, :])
        by_column = jnp.concatenate(column_sums + [jnp.zeros((LOCAL - HEADS, LOCAL), F32)], axis=0).T
        by_row = jnp.concatenate(row_sums + [jnp.zeros((LOCAL, LANES - HEADS), F32)], axis=1)
        r.dlogs[b, 0] = by_row - by_column * r.dt[l, here, :] + from_start
        r.dlogs[b, 1] = by_column
        yield
        exchange.turn()
        yield
        upper = (rows <= columns).astype(F32)
        strict = (rows > columns).astype(F32)
        ending = r.logs[l, (b + 1) * LOCAL - 1 : (b + 1) * LOCAL, :]
        tail = jnp.exp(ending - r.logs[l, here, :])
        tail_dt = dot(tail * r.dt[l, here, :], lanes, HIGHEST)
        ends = exchange.finish()
        ends_two = two(ends, 1)
        reach = dot_nt(twice(bs, 1), ends_two)
        xs = xs.astype(F32)
        pulled = dot_nt(xs * reach, lanes, HIGHEST) * tail
        r.dact[here, :INNER] += tail_dt * reach + skip * r.dy[here, :]
        r.dact[here, INNER : INNER + STATE] += product_of_two(two(xs * tail_dt, 1), ends_two)
        ones = jnp.ones((8, LANES), F32)
        starts = r.s0[l, b * INNER : (b + 1) * INNER, :]
        overlap = dot_nt(dot_nt(ones, ends * starts, HIGHEST), lanes, HIGHEST)[:1]
        dt = r.dt[l, here, :]
        dlas = (
            dot(upper, r.dlogs[b, 0], HIGHEST) + dot(strict, pulled * dt, HIGHEST) + overlap * jnp.exp(ending)
        )
        rate = -jnp.exp(head_row(r.decay_log, l))
        dstep = (r.dlogs[b, 1] + pulled + dlas * rate) * r.sig[l, here, :]
        r.dproj[l, here, INNER + CONV :] = dstep.astype(LOW)
        before = r.pre[l, here, :]
        opened = jax.nn.sigmoid(before)
        dbefore = r.dact[here, :] * opened * (1.0 + before * (1.0 - opened))
        r.dpre[b, 0:LOCAL, :] = dbefore
        r.edge[l, b] = dbefore[0:8]
        edge = mail.copy(r.edge.at[l, b], r.edge_seen.at[l, b], place.along_seq(-1))
        self.add_small(l, 6, jnp.sum(dstep, axis=0, keepdims=True))
        self.add_small(l, 7, jnp.sum(dlas * dt, axis=0, keepdims=True) * rate)
        self.add_small(l, 8, jnp.sum(dbefore, axis=0, keepdims=True))
        for tap in range(4):
            shifted = r.raw[l, b, 5 + tap : 5 + tap + LOCAL, :]
            self.add_small(l, 13 + 5 * tap, jnp.sum(dbefore * shifted, axis=0, keepdims=True))
        r.part[here, :] = dot_nt(r.dproj[l, here, :INNER], r.inner[l, 0]) + dot(
            r.dproj[l, here, INNER + CONV : INNER + CONV + HEADS], r.step[l]
        )
        yield
        edge.wait_recv()
        r.dpre[b, LOCAL:, :] = jnp.where(place.s == SEQ - 1, 0.0, r.edge_seen[l, b])
        draw = jnp.zeros((LOCAL, CONV), F32)
        for tap in range(4):
            draw += self.taps(l, tap) * r.dpre[b, 3 - tap : 3 - tap + LOCAL, :]
        r.dproj[l, here, INNER : INNER + CONV] = draw.astype(LOW)
        r.state_part[l, :, here] = draw[:, INNER:].T
        r.part[here, :] += dot_nt(r.dproj[l, here, INNER : 2 * INNER], r.inner[l, 1]) + dot_nt(
            r.dproj[l, here, 2 * INNER : INNER + CONV], r.state[l]
        )

    def backward_sum(self, l, b):
        r = self.r

        def finalize(dnormed, mine):
            rows = r.res[l, mine, :]
            factor = rms_factor(rows)
            u = rows * factor
            self.add_small(l, 33, jnp.sum(dnormed * u, axis=0, keepdims=True))
            du = dnormed * row(r.norm_gain, l)
            return r.grad[l + 1, mine, :] + factor * (du - u * jnp.mean(du * u, axis=-1, keepdims=True))

        return self.head_summing(l, b, r.part, self.wide(), r.grad.at[l], finalize)


    def weight_chunk(self, l, chunk):
        r, place, mail = self.r, self.place, self.mail
        own, flows = r.own, (0, 1)

        def blocks(flow, at, first, count):
            rows = pl.ds(flow * HALF + first, count)
            if flow == 0:
                return (chunk, slice(None), at, rows, slice(None))
            return (chunk, at, slice(None), rows, slice(None))

        def move(flow, steps):
            return place.along_x(steps) if flow == 0 else place.along_y(steps)

        def at_of(flow, steps):
            return place.x_at(steps) if flow == 0 else place.y_at(steps)

        def slot(flow):
            return chunk * 2 + flow

        posted = []

        def post(src, dst, to):
            posted.append(mail.copy(src, dst, to))
            return posted[-1]

        for k in range(RING):
            cols = slice(k * INNER, (k + 1) * INNER)
            if chunk == 0:
                value = dot_tn(r.grad_low[l, :, cols], r.mixed[l])
            else:
                value = dot_tn(r.normed[l, :, cols], r.dproj[l, :, (chunk - 1) * INNER : chunk * INNER])
            own[chunk, k] = value.reshape(RING, BLOCK, INNER)
        first, last = pl.ds(0, QUARTER), pl.ds(QUARTER, QUARTER)
        distant, near = {}, {}

        def parts(ref, flow, rows):
            return ref.at[slot(flow), :, rows]

        for flow in flows:
            far = at_of(flow, 2)
            distant[flow] = (
                post(own.at[blocks(flow, far, 0, QUARTER)], r.a1p.at[slot(flow)], move(flow, 1)),
                post(own.at[blocks(flow, far, QUARTER, QUARTER)], r.a1n.at[slot(flow)], move(flow, -1)),
            )
        for flow in flows:
            up, down = at_of(flow, 1), at_of(flow, -1)
            near[flow] = [
                post(own.at[blocks(flow, up, QUARTER, QUARTER)], parts(r.a2p, flow, last), move(flow, 1)),
                post(own.at[blocks(flow, down, 0, QUARTER)], parts(r.a2n, flow, first), move(flow, -1)),
            ]
        yield
        for flow in flows:
            up, down = at_of(flow, 1), at_of(flow, -1)
            for message in distant[flow]:
                message.wait_recv()
            own[blocks(flow, up, 0, QUARTER)] += r.a1p[slot(flow)]
            own[blocks(flow, down, QUARTER, QUARTER)] += r.a1n[slot(flow)]
            near[flow] += [
                post(own.at[blocks(flow, up, 0, QUARTER)], parts(r.a2p, flow, first), move(flow, 1)),
                post(own.at[blocks(flow, down, QUARTER, QUARTER)], parts(r.a2n, flow, last), move(flow, -1)),
            ]
        yield
        for flow in flows:
            k = slot(flow)
            for message in near[flow]:
                message.wait_recv()
            r.asum[k] = own[blocks(flow, at_of(flow, 0), 0, HALF)] + r.a2p[k] + r.a2n[k]
            other = 1 - flow
            far, up, down = at_of(other, 2), at_of(other, 1), at_of(other, -1)
            distant[flow] = (
                post(r.asum.at[k, far, first], r.a3p.at[k], move(other, 1)),
                post(r.asum.at[k, far, last], r.a3n.at[k], move(other, -1)),
            )
            near[flow] = [
                post(r.asum.at[k, up, last], r.a4p.at[k, last], move(other, 1)),
                post(r.asum.at[k, down, first], r.a4n.at[k, first], move(other, -1)),
            ]
        yield
        for flow in flows:
            k = slot(flow)
            other = 1 - flow
            up, down = at_of(other, 1), at_of(other, -1)
            for message in distant[flow]:
                message.wait_recv()
            r.asum[k, up, 0:QUARTER] += r.a3p[k]
            r.asum[k, down, QUARTER:HALF] += r.a3n[k]
            near[flow] += [
                post(r.asum.at[k, up, first], r.a4p.at[k, first], move(other, 1)),
                post(r.asum.at[k, down, last], r.a4n.at[k, last], move(other, -1)),
            ]
        yield
        for flow in flows:
            k = slot(flow)
            for message in near[flow]:
                message.wait_recv()
            value = r.asum[k, at_of(1 - flow, 0)] + r.a4p[k] + r.a4n[k]
            rows = slice(flow * HALF, (flow + 1) * HALF)
            if chunk == 0:
                r.output_grad[l, rows, :] = value
            else:
                r.pair_grad[l, chunk - 1, rows, :] = value
        for message in posted:
            message.done()

    def spread(self, src, dst, l, sems, slots):
        place = self.place

        def message(k):
            to = place.seq(k)
            return pltpu.make_async_remote_copy(
                src_ref=src(to) if slots is None else src.at[to] if slots else src,
                dst_ref=dst.at[place.s],
                send_sem=sems[0].at[l, k],
                recv_sem=sems[1].at[l, k],
                device_id=(to, place.h),
                device_id_type=MESH,
            )

        def each(what):
            def body(k, carry):
                what(message(k))
                return carry

            return lambda: lax.fori_loop(1, SEQ, body, 0)

        each(lambda m: m.start())()
        return each(lambda m: m.wait_recv()), each(lambda m: m.wait_send())

    def to_heads(self, src, dst, slots):
        place, mail = self.place, self.mail
        sent = []
        for k in range(1, HEAD):
            to = lax.rem(place.h + k, HEAD)
            piece = src.at[pl.ds(pl.multiple_of(to * PART, PART), PART)] if slots else src
            sent.append(mail.copy(piece, dst.at[place.h], (place.s, to)))
        return sent

    def state_weights(self, l):
        r, place = self.r, self.place
        sent = self.to_heads(r.state_part.at[l], r.state_seen.at[l], True)
        yield
        total = r.state_part[l, pl.ds(pl.multiple_of(place.h * PART, PART), PART), :]
        for k in range(1, HEAD):
            sent[k - 1].wait_recv()
        for k in range(1, HEAD):
            total = total + r.state_seen[l, lax.rem(place.h + k, HEAD)]
        steps = r.dproj[l, :, INNER + CONV :].astype(F32).T[0:8]
        both = jnp.concatenate([total, steps], axis=0).astype(LOW)
        for k in range(RING):
            product = dot(both, r.normed[l, :, k * INNER : (k + 1) * INNER])
            for j in range(RING):
                owner = k * RING + j
                r.misc[l, owner, :, 0:BLOCK] = product[:, j * BLOCK : (j + 1) * BLOCK]
        r.misc_seen[l, place.s] = r.misc[l, place.s]
        scattered = self.spread(r.misc.at[l], r.misc_seen.at[l], l, (r.scatter_send, r.scatter_recv), True)
        yield
        scattered[0]()
        total = r.misc_seen[l, 0]
        for k in range(1, SEQ):
            total = total + r.misc_seen[l, k]
        r.step_grad[l] = total[PART:]
        r.shared[l] = total[0:PART]
        r.state_grad[l, place.h] = total[0:PART]
        sent = self.to_heads(r.shared.at[l], r.shared_seen.at[l], False)
        yield
        for message in sent:
            message.wait_recv()
        for k in range(1, HEAD):
            at = lax.rem(place.h + k, HEAD)
            r.state_grad[l, at] = r.shared_seen[l, at]
        scattered[1]()

    def small_sums(self, l):
        r, place = self.r, self.place
        r.tiny_seen[l, place.s] = r.small[l, pl.ds(pl.multiple_of(place.s * SMALL_PIECE, 8), SMALL_PIECE), :]

        def piece(to):
            return r.small.at[l, pl.ds(pl.multiple_of(to * SMALL_PIECE, 8), SMALL_PIECE)]

        scattered = self.spread(piece, r.tiny_seen.at[l], l, (r.tiny_send, r.tiny_recv), None)
        yield
        scattered[0]()
        total = r.tiny_seen[l, 0]
        for k in range(1, SEQ):
            total = total + r.tiny_seen[l, k]
        r.tiny[l] = total
        sent = self.to_heads(r.tiny.at[l], r.tiny_heads.at[l], False)
        yield
        for message in sent:
            message.wait_recv()
        over_head = total
        for k in range(1, HEAD):
            over_head = over_head + r.tiny_heads[l, lax.rem(place.h + k, HEAD)]
        at = lax.broadcasted_iota(jnp.int32, (SMALL_PIECE, LANES), 0) + place.s * SMALL_PIECE
        joint = at < 0
        for low, high in SHARED:
            joint = joint | ((at >= low) & (at < high))
        r.small_seen[l, place.s] = jnp.where(joint, over_head, total)
        gathered = self.spread(
            r.small_seen.at[l, place.s], r.small_seen.at[l], l, (r.gather_send, r.gather_recv), False
        )
        yield
        gathered[0]()
        r.small_out[l] = r.small_seen[l]
        gathered[1]()
        scattered[1]()


FORWARD, FORWARD_SUM, FORWARD_DONE, BACKWARD, BACKWARD_SUM, BACKWARD_DONE = range(6)


def chain(program, b):
    for l in range(LAYERS):
        for step, _ in enumerate(program.forward(l, b)):
            yield FORWARD, l, step
        if l < LAYERS - 1:
            for step, _ in enumerate(program.forward_sum(l, b)):
                yield FORWARD_SUM, l, step
        else:
            yield FORWARD_DONE, l, 0
    for l in reversed(range(LAYERS)):
        for step, _ in enumerate(program.backward(l, b)):
            yield BACKWARD, l, step
        for step, _ in enumerate(program.backward_sum(l, b)):
            yield BACKWARD_SUM, l, step
        yield BACKWARD_DONE, l, 0


def last(b):
    return Program.forward_sum, LAYERS - 1, b


def chunk(l, k):
    return Program.weight_chunk, l, k


def state(l):
    return Program.state_weights, l


def small(l):
    return Program.small_sums, l


STORE = (Program.store,)

BEHIND = {
    (FORWARD_DONE, 1, 0, 0): (last(0),),
    (FORWARD_DONE, 1, 0, 1): (last(1),),
    (BACKWARD, 1, 0, 0): (last(0),),
    (BACKWARD, 1, 0, 1): (last(1),),
    (BACKWARD, 1, 1, 0): (last(0),),
    (BACKWARD, 1, 1, 1): (last(1),),
    (BACKWARD, 1, 2, 0): (last(0),),
    (BACKWARD, 1, 2, 1): (last(1), chunk(1, 0)),
    (BACKWARD, 1, 3, 0): (last(0),),
    (BACKWARD, 1, 3, 1): (last(1), chunk(1, 1)),
    (BACKWARD_SUM, 1, 0, 0): (last(0),),
    (BACKWARD_SUM, 1, 0, 1): (last(1), state(1), chunk(1, 0), chunk(1, 2)),
    (BACKWARD_SUM, 1, 1, 0): (last(0),),
    (BACKWARD_SUM, 1, 1, 1): (last(1), chunk(1, 1)),
    (BACKWARD_SUM, 1, 2, 1): (state(1), chunk(1, 0)),
    (BACKWARD_SUM, 1, 3, 1): (chunk(1, 1), chunk(1, 2)),
    (BACKWARD_SUM, 1, 4, 1): (chunk(1, 0),),
    (BACKWARD_SUM, 1, 5, 1): (state(1), chunk(1, 1)),
    (BACKWARD_DONE, 1, 0, 1): (STORE, chunk(1, 0), chunk(1, 2)),
    (BACKWARD, 0, 0, 1): (chunk(1, 1), chunk(1, 2)),
    (BACKWARD, 0, 1, 1): (state(1), small(1), chunk(1, 2)),
    (BACKWARD, 0, 2, 1): (chunk(0, 0),),
    (BACKWARD, 0, 3, 1): (chunk(0, 0), chunk(0, 1)),
    (BACKWARD_SUM, 0, 0, 1): (state(0), small(1), chunk(0, 0), chunk(0, 1), chunk(0, 2)),
    (BACKWARD_SUM, 0, 1, 1): (state(0), chunk(0, 1)),
    (BACKWARD_SUM, 0, 2, 1): (small(1), chunk(0, 0), chunk(0, 2)),
    (BACKWARD_SUM, 0, 3, 1): (small(0), state(0), chunk(0, 1), chunk(0, 0)),
    (BACKWARD_SUM, 0, 4, 1): (small(0), chunk(0, 2), chunk(0, 1)),
    (BACKWARD_SUM, 0, 5, 1): (small(0), state(0), small(1), chunk(0, 2)),
    (BACKWARD_DONE, 0, 0, 1): (small(0), chunk(0, 2)),
}


def whole_kernel(names, *refs):
    r = SimpleNamespace(**dict(zip(names, refs)))
    program = Program(r)
    place = program.place
    barrier = greet(
        [place.along_seq(k) for k in range(1, SEQ)] + [place.along_head(k) for k in range(1, HEAD)]
    )
    program.start_loads()
    r.small[...] = jnp.zeros_like(r.small)
    r.misc[...] = jnp.zeros_like(r.misc)
    steps = r.step_in[...].astype(F32)
    for l in range(LAYERS):
        r.step[l] = steps[:, l, :].astype(LOW)
    program.barrier = barrier
    tasks = {}

    def go_on(task):
        if task not in tasks:
            tasks[task] = task[0](program, *task[1:])
        if next(tasks[task], StopIteration) is StopIteration:
            tasks[task] = iter(())

    live = {b: chain(program, b) for b in range(SEQS)}
    while live:
        for b in list(live):
            at = next(live[b], None)
            if at is None:
                del live[b]
                continue
            for name in BEHIND.get((*at, b), ()):
                go_on(name)
    program.put(r.grad.at[0], r.hidden_grad)
    for task in list(tasks) * 8:
        go_on(task)
    for copy in program.stores:
        copy.wait()
    program.mail.finish()


def floats(*shape):
    return pltpu.VMEM(shape, F32)


def lows(*shape):
    return pltpu.VMEM(shape, LOW)


def dma(*shape):
    return pltpu.SemaphoreType.DMA(shape)


def run(args):
    inputs = dict(
        hidden_in=pl.ANY,
        cotangent_in=pl.ANY,
        norm_gain=pltpu.VMEM,
        inner_in=pl.ANY,
        state_in=pl.ANY,
        step_in=pltpu.VMEM,
        conv_weight=pltpu.VMEM,
        conv_bias=pltpu.VMEM,
        conv_state_weight=pltpu.VMEM,
        conv_state_bias=pltpu.VMEM,
        step_bias=pltpu.VMEM,
        decay_log=pltpu.VMEM,
        skip_gain=pltpu.VMEM,
        mixer_gain=pltpu.VMEM,
        output_in=pl.ANY,
    )
    outputs = dict(
        hidden_out=((SEQS, LOCAL, WIDTH), pl.ANY),
        hidden_grad=((SEQS, LOCAL, WIDTH), pl.ANY),
        pair_grad=((LAYERS, 2, BLOCK, INNER), pltpu.VMEM),
        state_grad=((LAYERS, HEAD, PART, LANES), pltpu.VMEM),
        step_grad=((LAYERS, 8, LANES), pltpu.VMEM),
        small_out=((LAYERS, SEQ, SMALL_PIECE, LANES), pltpu.VMEM),
        output_grad=((LAYERS, BLOCK, INNER), pltpu.VMEM),
    )
    flows = 2 * CHUNKS
    copies = (
        (2 * LAYERS + 2 * LAYERS) * HEAD_SUM_COPIES
        + LAYERS * SEQS * (2 + HEAD - 1)
        + 3 * LAYERS * (HEAD - 1)
        + LAYERS * flows * 12
    )
    scratch = dict(
        res=floats(LAYERS + 1, ROWS, WIDTH),
        grad=floats(LAYERS + 1, ROWS, WIDTH),
        inner=lows(LAYERS, 2, WIDTH, INNER),
        state=lows(LAYERS, WIDTH, 2 * STATE),
        step=lows(LAYERS, HEADS, WIDTH),
        wout=lows(LAYERS, WIDTH, INNER),
        normed=lows(LAYERS, ROWS, WIDTH),
        gate=floats(LAYERS, ROWS, INNER),
        raw=floats(LAYERS, SEQS, 8 + LOCAL, CONV),
        pre=floats(LAYERS, ROWS, CONV),
        act=lows(LAYERS, ROWS, CONV),
        dt=floats(LAYERS, ROWS, LANES),
        logs=floats(LAYERS, ROWS, LANES),
        sig=floats(LAYERS, ROWS, LANES),
        y=floats(LAYERS, ROWS, INNER),
        s0=floats(LAYERS, SEQS * INNER, STATE),
        factor=floats(LAYERS, ROWS, LANES),
        means=floats(ROWS, LANES),
        dmixed=floats(ROWS, INNER),
        gated=floats(ROWS, INNER),
        sums=floats(LAYERS, SEQS, 8, LOCAL),
        sums_seen=floats(LAYERS, SEQS, HEAD, 8, LOCAL),
        halo=floats(LAYERS, SEQS, 8, WIDTH),
        part=floats(ROWS, WIDTH),
        pair=floats(SEQS, HALVED, WIDTH),
        half_p=floats(SEQS, SHARE // 2, WIDTH),
        half_n=floats(SEQS, SHARE // 2, WIDTH),
        near_p=floats(SEQS, SHARE, WIDTH),
        near_n=floats(SEQS, SHARE, WIDTH),
        last_part=floats(ROWS, WIDTH),
        last_pair=floats(SEQS, HALVED, WIDTH),
        last_half_p=floats(SEQS, SHARE // 2, WIDTH),
        last_half_n=floats(SEQS, SHARE // 2, WIDTH),
        last_near_p=floats(SEQS, SHARE, WIDTH),
        last_near_n=floats(SEQS, SHARE, WIDTH),
        state_part=floats(LAYERS, 2 * STATE, ROWS),
        state_seen=floats(LAYERS, HEAD, PART, ROWS),
        stage=floats(SEQ, PIECE + 8, LANES),
        seen=floats(SEQ, PIECE + 8, LANES),
        kept=floats(LAYERS, SEQ, 8, LANES),
        turned=floats(SEQ, PIECE, LANES),
        back=floats(SEQ, PIECE, LANES),
        grad_low=lows(LAYERS, ROWS, WIDTH),
        mixed=lows(LAYERS, ROWS, INNER),
        dproj=lows(LAYERS, ROWS, PROJ),
        dy=floats(ROWS, INNER),
        dact=floats(ROWS, CONV),
        dlogs=floats(SEQS, 2, LOCAL, LANES),
        dpre=floats(SEQS, LOCAL + 8, CONV),
        edge=floats(LAYERS, SEQS, 8, CONV),
        edge_seen=floats(LAYERS, SEQS, 8, CONV),
        small=floats(LAYERS, SMALL, LANES),
        own=floats(CHUNKS, RING, RING, BLOCK, INNER),
        a1p=floats(flows, RING, QUARTER, INNER),
        a1n=floats(flows, RING, QUARTER, INNER),
        a2p=floats(flows, RING, HALF, INNER),
        a2n=floats(flows, RING, HALF, INNER),
        asum=floats(flows, RING, HALF, INNER),
        a3p=floats(flows, QUARTER, INNER),
        a3n=floats(flows, QUARTER, INNER),
        a4p=floats(flows, HALF, INNER),
        a4n=floats(flows, HALF, INNER),
        misc=floats(LAYERS, SEQ, MISC, LANES),
        misc_seen=floats(LAYERS, SEQ, MISC, LANES),
        shared=floats(LAYERS, PART, LANES),
        shared_seen=floats(LAYERS, HEAD, PART, LANES),
        tiny=floats(LAYERS, SMALL_PIECE, LANES),
        tiny_seen=floats(LAYERS, SEQ, SMALL_PIECE, LANES),
        tiny_heads=floats(LAYERS, HEAD, SMALL_PIECE, LANES),
        small_seen=floats(LAYERS, SEQ, SMALL_PIECE, LANES),
        mail_send=dma(copies),
        mail_recv=dma(copies),
        leg1_send=dma(SEQ),
        leg1_recv=dma(SEQ),
        leg2_send=dma(SEQ),
        leg2_recv=dma(SEQ),
        scatter_send=dma(LAYERS, SEQ),
        scatter_recv=dma(LAYERS, SEQ),
        tiny_send=dma(LAYERS, SEQ),
        tiny_recv=dma(LAYERS, SEQ),
        gather_send=dma(LAYERS, SEQ),
        gather_recv=dma(LAYERS, SEQ),
        load=dma(2 * SEQS + 4 * LAYERS),
        store=dma(2 * SEQS),
    )
    results = pl.pallas_call(
        partial(whole_kernel, list(inputs) + list(outputs) + list(scratch)),
        out_shape=[jax.ShapeDtypeStruct(shape, F32) for shape, _ in outputs.values()],
        in_specs=[pl.BlockSpec(memory_space=space) for space in inputs.values()],
        out_specs=[pl.BlockSpec(memory_space=space) for _, space in outputs.values()],
        scratch_shapes=list(scratch.values()),
        compiler_params=pltpu.CompilerParams(
            collective_id=0, has_side_effects=True, vmem_limit_bytes=VMEM_LIMIT
        ),
    )(*args)
    return SimpleNamespace(**dict(zip(outputs, results)))


def pack_kernel(
    whole_out,
    whole_grad,
    pair_in,
    state_in,
    step_in,
    small,
    output_in,
    hidden_out,
    hidden_grad,
    norm_gain,
    pair,
    state,
    step,
    conv_weight,
    conv_bias,
    conv_state_weight,
    conv_state_bias,
    step_bias,
    decay_log,
    skip_gain,
    mixer_gain,
    output,
):
    hidden_out[...] = whole_out[...]
    hidden_grad[...] = whole_grad[...]
    output[...] = output_in[...]

    def lanes(l, first, count):
        rows = [small[l, (first + k) // 8, (first + k) % 8 : (first + k) % 8 + 1, :] for k in range(count)]
        return jnp.concatenate(rows, axis=1)

    for l in range(LAYERS):
        one = slice(l, l + 1)
        for part in range(2):
            pair[l, :, part, :] = pair_in[l, part]
        columns = state_in[l].reshape(2 * STATE, LANES)
        for half in range(2):
            cols = slice(half * STATE, (half + 1) * STATE)
            state[l, :, cols] = columns[cols].T[:BLOCK]
        norm_gain[one, :] = lanes(l, 33, 12)
        for head in range(HEADS):
            step[head, one, :] = step_in[l, head : head + 1, :BLOCK]
        for tap in range(4):
            conv_weight[l, tap : tap + 1, :] = lanes(l, 13 + 5 * tap, 3)
            conv_state_weight[l, tap : tap + 1, :] = lanes(l, 16 + 5 * tap, 2)
        conv_bias[one, :] = lanes(l, 8, 3)
        conv_state_bias[one, :] = lanes(l, 11, 2)
        step_bias[one, :] = lanes(l, 6, 1)[:, :HEADS]
        decay_log[one, :] = lanes(l, 7, 1)[:, :HEADS]
        skip = dot_nt(jnp.broadcast_to(lanes(l, 3, 3), (8, INNER)), head_lanes(), HIGHEST)
        skip_gain[one, :] = skip[0:1, :HEADS]
        mixer_gain[one, :] = lanes(l, 0, 3)


def shards(*args):
    args = list(args)
    args[3] = args[3].transpose(0, 2, 1, 3)
    args[5] = args[5].transpose(2, 0, 1)
    out = run(args)
    big = (SEQS, LOCAL, WIDTH)
    shapes = [
        big,
        big,
        (LAYERS, WIDTH),
        (LAYERS, BLOCK, 2, INNER),
        (LAYERS, BLOCK, 2 * STATE),
        (HEADS, LAYERS, BLOCK),
        (LAYERS, 4, INNER),
        (LAYERS, INNER),
        (LAYERS, 4, 2 * STATE),
        (LAYERS, 2 * STATE),
        (LAYERS, HEADS),
        (LAYERS, HEADS),
        (LAYERS, HEADS),
        (LAYERS, INNER),
        (LAYERS, BLOCK, INNER),
    ]
    held = [pl.BlockSpec(memory_space=pltpu.VMEM)]
    packed = list(
        pl.pallas_call(
            pack_kernel,
            out_shape=[jax.ShapeDtypeStruct(shape, F32) for shape in shapes],
            in_specs=held * 7,
            out_specs=held * 15,
        )(
            out.hidden_out,
            out.hidden_grad,
            out.pair_grad,
            out.state_grad,
            out.step_grad,
            out.small_out,
            out.output_grad,
        )
    )
    packed[5] = packed[5].transpose(1, 2, 0)
    return tuple(packed)


def solution(mesh):
    heads = P(None, None, "head")
    in_specs = (
        P(None, "seq", None),
        P(None, "seq", None),
        P(),
        P(None, None, None, "head"),
        P(),
        heads,
        heads,
        P(None, "head"),
        P(),
        P(),
        P(None, "head"),
        P(None, "head"),
        P(None, "head"),
        P(None, "head"),
        heads,
    )
    out_specs = (
        P(None, "seq", None),
        P(None, "seq", None),
        P(),
        P(None, "seq", None, "head"),
        P(None, "seq", None),
        P(None, "seq", "head"),
        heads,
        P(None, "head"),
        P(),
        P(),
        P(None, "head"),
        P(None, "head"),
        P(None, "head"),
        P(None, "head"),
        P(None, "seq", "head"),
    )
    return jax.shard_map(shards, mesh=mesh, in_specs=in_specs, out_specs=out_specs, check_vma=False)
```

```python
from types import SimpleNamespace

from functools import partial

import jax
import jax.numpy as jnp
from jax import lax
from jax.experimental import pallas as pl
from jax.experimental.pallas import tpu as pltpu
from jax.sharding import PartitionSpec as P

MESH = pl.DeviceIdType.MESH
HIGHEST = lax.Precision.HIGHEST
EPSILON = 1e-05
F32 = jnp.float32
LOW = jnp.bfloat16

RING = 4
SEQ = 16
HEAD = 8
SEQS = 2
LOCAL = 128
ROWS = SEQS * LOCAL
WIDTH = 1536
INNER = 384
TOTAL = 3072
HEADS = 6
STATE = 128
CONV = INNER + 2 * STATE
PROJ = 2 * INNER + 2 * STATE + 128
LANES = 128
PIECE = SEQS * INNER // SEQ
OWNERS = SEQ // SEQS
GROUPS = PIECE // 16
LAYERS = 2
HALVED = LOCAL // 2
SHARE = LOCAL // HEAD
BLOCK = WIDTH // SEQ
VMEM_LIMIT = 63 * 1024 * 1024


def dot(a, b, precision=None):
    return lax.dot_general(a, b, (((1,), (0,)), ((), ())), precision=precision, preferred_element_type=F32)


def dot_nt(a, b, precision=None):
    return lax.dot_general(a, b, (((1,), (1,)), ((), ())), precision=precision, preferred_element_type=F32)


def dot_tn(a, b, precision=None):
    return lax.dot_general(a, b, (((0,), (0,)), ((), ())), precision=precision, preferred_element_type=F32)


class Place:
    def __init__(self):
        self.s = lax.axis_index("seq")
        self.h = lax.axis_index("head")
        self.x, self.y = lax.rem(self.s, RING), lax.div(self.s, RING)
        self.core, self.z = lax.rem(self.h, 2), lax.div(self.h, 2)

    def seq(self, steps):
        return lax.rem(self.s + steps + SEQ, SEQ)

    def along_seq(self, steps):
        return (self.seq(steps), self.h)

    def along_head(self, steps):
        return (self.s, lax.rem(self.h + steps, HEAD))

    def partner(self):
        return (self.s, self.h + 1 - 2 * self.core)

    def x_at(self, steps):
        return lax.rem(self.x + steps + RING, RING)

    def y_at(self, steps):
        return lax.rem(self.y + steps + RING, RING)

    def z_at(self, steps):
        return lax.rem(self.z + steps + RING, RING)

    def along_x(self, steps):
        return (self.y * RING + self.x_at(steps), self.h)

    def along_y(self, steps):
        return (self.y_at(steps) * RING + self.x, self.h)

    def along_z(self, steps):
        return (self.s, self.z_at(steps) * 2 + self.core)


class Message:
    def __init__(self, copy):
        self.copy, self.out = copy, True

    def wait_recv(self):
        self.copy.wait_recv()

    def done(self):
        if self.out:
            self.copy.wait_send()
            self.out = False


class Mail:
    def __init__(self, send, recv):
        self.send, self.recv, self.sent = send, recv, []

    def copy(self, src, dst, to):
        at = len(self.sent)
        copy = pltpu.make_async_remote_copy(
            src_ref=src,
            dst_ref=dst,
            send_sem=self.send.at[at],
            recv_sem=self.recv.at[at],
            device_id=to,
            device_id_type=MESH,
        )
        copy.start()
        self.sent.append(Message(copy))
        return self.sent[-1]

    def finish(self):
        for message in self.sent:
            message.done()


def greet(peers):
    barrier = pltpu.get_barrier_semaphore()
    for peer in peers:
        pl.semaphore_signal(barrier, inc=1, device_id=peer, device_id_type=MESH)
    return barrier


def masks():
    row = lax.broadcasted_iota(jnp.int32, (LOCAL, LOCAL), 0)
    column = lax.broadcasted_iota(jnp.int32, (LOCAL, LOCAL), 1)
    return row, column


def head_lanes():
    head = lax.broadcasted_iota(jnp.int32, (LANES, INNER), 0)
    channel = lax.broadcasted_iota(jnp.int32, (LANES, INNER), 1)
    return (lax.div(channel, INNER // HEADS) == head).astype(F32)


def split_pair(pair):
    first = lax.broadcasted_iota(jnp.int32, (LOCAL, LANES), 1) < LANES // 2
    zero = jnp.zeros_like(pair)
    return jnp.concatenate([jnp.where(first, pair, zero), jnp.where(first, zero, pair)], axis=0)


def two(values, axis):
    high = values.astype(LOW)
    return jnp.concatenate([high, (values - high.astype(F32)).astype(LOW)], axis=axis)


def twice(values, axis):
    return jnp.concatenate([values, values], axis=axis)


def product_of_two(a, b):
    high, low = b[:, :STATE], b[:, STATE:]
    return dot(a, twice(high, 0)) + dot(a[:, :INNER], low)


def rms_factor(rows):
    return lax.rsqrt(jnp.mean(rows * rows, axis=-1, keepdims=True) + EPSILON)


def head_row(ref, layer):
    return jnp.concatenate([ref[layer : layer + 1, :], jnp.zeros((1, LANES - HEADS), F32)], axis=1)


def row(ref, layer):
    return ref[layer : layer + 1, :]


def seq_rows(at):
    return slice(at * LOCAL, (at + 1) * LOCAL)


def head_sum(place, mail, part, pair, half_p, half_n, near_p, near_n, whole, first_row, finalize):
    core, z = place.core, place.z
    half = SHARE // 2

    def rows(of_core, of_z, first=0, count=SHARE):
        return pl.ds(pl.multiple_of(first_row + of_core * HALVED + of_z * SHARE + first, 8), count)

    def pair_rows(of_z):
        return pl.ds(pl.multiple_of(of_z * SHARE, 8), SHARE)

    partner, above_to, below_to = place.partner(), place.along_z(1), place.along_z(-1)
    posted = []

    def post(src, dst, to):
        posted.append(mail.copy(src, dst, to))
        return posted[-1]

    swapped = {}
    for step in (2, 1, 3, 0):
        at = place.z_at(step)
        swapped[step] = post(part.at[rows(1 - core, at)], pair.at[pair_rows(at)], partner)
    yield

    def join(step):
        at = place.z_at(step)
        swapped[step].wait_recv()
        part[rows(core, at), :] += pair[pair_rows(at), :]

    join(2)
    far, above, below = place.z_at(2), place.z_at(1), place.z_at(-1)
    first, last = pl.ds(0, half), pl.ds(half, half)
    up = post(part.at[rows(core, far, 0, half)], half_p, above_to)
    down = post(part.at[rows(core, far, half, half)], half_n, below_to)
    join(1)
    near = [post(part.at[rows(core, above, half, half)], near_p.at[last], above_to)]
    join(3)
    near.append(post(part.at[rows(core, below, 0, half)], near_n.at[first], below_to))
    join(0)
    yield
    up.wait_recv()
    part[rows(core, above, 0, half), :] += half_p[...]
    near.append(post(part.at[rows(core, above, 0, half)], near_p.at[first], above_to))
    down.wait_recv()
    part[rows(core, below, half, half), :] += half_n[...]
    near.append(post(part.at[rows(core, below, half, half)], near_n.at[last], below_to))
    yield
    for message in near:
        message.wait_recv()
    mine = rows(core, z)
    whole[mine, :] = finalize(part[mine, :] + near_p[...] + near_n[...], mine)
    up = post(whole.at[mine], whole.at[mine], above_to)
    down = post(whole.at[mine], whole.at[mine], below_to)
    across = [post(whole.at[mine], whole.at[mine], partner)]
    yield
    up.wait_recv()
    piece = rows(core, below, 0, half)
    up = post(whole.at[piece], whole.at[piece], above_to)
    piece = rows(core, below)
    across.append(post(whole.at[piece], whole.at[piece], partner))
    down.wait_recv()
    piece = rows(core, above, half, half)
    down = post(whole.at[piece], whole.at[piece], below_to)
    piece = rows(core, above)
    across.append(post(whole.at[piece], whole.at[piece], partner))
    yield
    up.wait_recv()
    piece = rows(core, far, 0, half)
    across.append(post(whole.at[piece], whole.at[piece], partner))
    down.wait_recv()
    piece = rows(core, far, half, half)
    across.append(post(whole.at[piece], whole.at[piece], partner))
    yield
    for message in across:
        message.wait_recv()
    for message in posted:
        message.done()


HEAD_SUM_COPIES = 4 + 2 + 4 + 2 + 2 + 5


class Exchange:
    def __init__(self, place, r, l, at, reverse):
        self.place, self.r, self.l, self.at, self.reverse = place, r, l, at, reverse
        self.rows = pl.ds(0, PIECE if reverse else PIECE + 8)
        self.owner = lax.rem(place.x + place.y, SEQS) == at
        self.owners = [RING * y + x for y in range(RING) for x in range(RING) if (x + y) % SEQS == at]

    def to_owner(self, k):
        owner = self.owners[k]
        r, s = self.r, self.place.s
        return pltpu.make_async_remote_copy(
            src_ref=r.stage.at[owner, self.rows],
            dst_ref=r.seen.at[s, self.rows],
            send_sem=r.leg1_send.at[owner],
            recv_sem=r.leg1_recv.at[s],
            device_id=(owner, self.place.h),
            device_id_type=MESH,
        )

    def from_source(self, k):
        r, source = self.r, self.place.seq(k)
        return pltpu.make_async_remote_copy(
            src_ref=r.stage.at[source, self.rows],
            dst_ref=r.seen.at[source, self.rows],
            send_sem=r.leg1_send.at[source],
            recv_sem=r.leg1_recv.at[source],
            device_id=(source, self.place.h),
            device_id_type=MESH,
        )

    def to_device(self, k):
        r, s, to = self.r, self.place.s, self.place.seq(k)
        return pltpu.make_async_remote_copy(
            src_ref=r.turned.at[to],
            dst_ref=r.back.at[s],
            send_sem=r.leg2_send.at[to],
            recv_sem=r.leg2_recv.at[s],
            device_id=(to, self.place.h),
            device_id_type=MESH,
        )

    def from_owner(self, k):
        owner = self.owners[k]
        r = self.r
        return pltpu.make_async_remote_copy(
            src_ref=r.turned.at[owner],
            dst_ref=r.back.at[owner],
            send_sem=r.leg2_send.at[owner],
            recv_sem=r.leg2_recv.at[owner],
            device_id=(owner, self.place.h),
            device_id_type=MESH,
        )

    def each_owner(self, what):
        for k in range(OWNERS):

            @pl.when(self.owners[k] != self.place.s)
            def _(k=k):
                what(k)

    def start(self, state, decays=None):
        r = self.r
        for piece in range(OWNERS):
            slot = self.owners[piece]
            r.stage[slot, 0:PIECE, :] = state[piece * PIECE : (piece + 1) * PIECE]
            if self.reverse:
                continue
            for group in range(GROUPS):
                head = (piece * GROUPS + group) // 4
                r.stage[slot, PIECE + group : PIECE + group + 1, :] = decays[head]
            r.stage[slot, PIECE + GROUPS : PIECE + 8, :] = jnp.zeros((8 - GROUPS, LANES), F32)
        self.each_owner(lambda k: self.to_owner(k).start())

        @pl.when(self.owner)
        def _():
            r.seen[self.place.s] = r.stage[self.place.s]

    def turn(self):
        r = self.r

        @pl.when(self.owner)
        def _():
            def landed(k, carry):
                self.from_source(k).wait_recv()
                return carry

            lax.fori_loop(1, SEQ, landed, 0)
            if not self.reverse:
                r.kept[self.l] = r.seen[:, PIECE:, :]

            def hop(step, carry):
                at = SEQ - 1 - step if self.reverse else step
                for group in range(GROUPS):
                    r.turned[at, group * 16 : group * 16 + 16, :] = carry[group]
                return tuple(
                    r.kept[self.l, at, group : group + 1, :] * carry[group]
                    + r.seen[at, group * 16 : group * 16 + 16, :]
                    for group in range(GROUPS)
                )

            lax.fori_loop(0, SEQ, hop, tuple(jnp.zeros((16, LANES), F32) for _ in range(GROUPS)))

            def send(k, carry):
                self.to_device(k).start()
                return carry

            lax.fori_loop(1, SEQ, send, 0)
            r.back[self.place.s] = r.turned[self.place.s]

    def finish(self):
        self.each_owner(lambda k: self.from_owner(k).wait_recv())
        self.each_owner(lambda k: self.to_owner(k).wait_send())

        @pl.when(self.owner)
        def _():
            def left(k, carry):
                self.to_device(k).wait_send()
                return carry

            lax.fori_loop(1, SEQ, left, 0)

        return jnp.concatenate([self.r.back[owner] for owner in self.owners], axis=0)


SMALL = 128
SMALL_PIECE = SMALL // SEQ
PART = 2 * STATE // HEAD
MISC = PART + 8
SHARED = ((11, 13), (16, 18), (21, 23), (26, 28), (31, 33), (33, 45))
HALF = BLOCK // 2
QUARTER = BLOCK // 4
CHUNKS = 3


class Program:
    def __init__(self, r):
        self.r = r
        self.place = Place()
        self.mail = Mail(r.mail_send, r.mail_recv)
        self.loads = {}
        self.sums_sent = {}
        self.stores = []


    def load(self, name, src, dst):
        copy = pltpu.make_async_copy(src, dst, self.r.load.at[len(self.loads)])
        copy.start()
        self.loads[name] = copy

    def need(self, *names):
        for name in names:
            copy = self.loads.get(name)
            if copy is not None:
                copy.wait()
                self.loads[name] = None

    def load_weights(self, l):
        r = self.r
        self.load((1, l), r.inner_in.at[l], r.mingled)
        self.load((2, l), r.state_in.at[l], r.state.at[l])
        self.load((4, l), r.output_in.at[l], r.wout.at[l])

    def part(self, l, which):
        r = self.r

        def rows_of(at, carry):
            rows = pl.ds(pl.multiple_of(at * 64, 64), 64)
            r.inner[l, which, rows, :] = r.mingled[rows, which, :]
            return carry

        lax.fori_loop(0, WIDTH // 64, rows_of, 0)

    def part_next(self, l):
        self.need((1, l))
        self.part(l, 1)
        yield
        self.part(l, 0)

    def start_loads(self):
        r = self.r
        for b in range(SEQS):
            self.load((0, b), r.hidden_in.at[b], r.res.at[0, pl.ds(b * LOCAL, LOCAL)])
        self.load_weights(0)

    def more_loads(self):
        r = self.r
        for l in range(1, LAYERS):
            self.load_weights(l)
        for b in range(SEQS):
            self.load((5, b), r.cotangent_in.at[b], r.grad.at[LAYERS, pl.ds(b * LOCAL, LOCAL)])

    def put(self, source, target):
        for b in range(SEQS):
            copy = pltpu.make_async_copy(
                source.at[pl.ds(b * LOCAL, LOCAL)], target.at[b], self.r.store.at[len(self.stores)]
            )
            copy.start()
            self.stores.append(copy)

    def store(self):
        self.put(self.r.res.at[LAYERS], self.r.hidden_out)
        yield

    def head_summing(self, l, b, part, extra, whole, finalize):
        r = self.r
        pair, half_p, half_n, near_p, near_n = extra
        return head_sum(
            self.place,
            self.mail,
            part,
            pair.at[b],
            half_p.at[b],
            half_n.at[b],
            near_p.at[b],
            near_n.at[b],
            whole,
            b * LOCAL,
            finalize,
        )

    def wide(self):
        r = self.r
        return r.pair, r.half_p, r.half_n, r.near_p, r.near_n

    def last(self):
        r = self.r
        return r.last_pair, r.last_half_p, r.last_half_n, r.last_near_p, r.last_near_n

    def add_small(self, l, at, values):
        for k in range(values.shape[1] // LANES):
            self.r.small[l, at + k : at + k + 1, :] += values[:, k * LANES : (k + 1) * LANES]

    def taps(self, l, tap):
        r = self.r
        return jnp.concatenate([r.conv_weight[l, tap : tap + 1, :], r.conv_state_weight[l, tap : tap + 1, :]], axis=1)

    def decays(self, l, b):
        r = self.r
        decay = jnp.exp(r.logs[l, (b + 1) * LOCAL - 1 : (b + 1) * LOCAL, :])
        return [jnp.broadcast_to(decay[:, h : h + 1], (1, LANES)) for h in range(HEADS)]

    def pass_on(self, l, b):
        rows = self.r.res.at[l, pl.ds((b + 1) * LOCAL - 8, 8)]
        return self.mail.copy(rows, self.r.halo.at[l, b], self.place.along_seq(1))

    def forward(self, l, b):
        r, place, mail = self.r, self.place, self.mail
        here = seq_rows(b)
        gain = row(r.norm_gain, l)
        self.need((0, b))

        def norm_rows(at, carry):
            rows = pl.ds(pl.multiple_of(b * LOCAL + at * 32, 32), 32)
            values = r.res[l, rows, :]
            r.normed[l, rows, :] = (values * rms_factor(values) * gain).astype(LOW)
            return carry

        if l > 0:
            edge = self.pass_on(l, b)
        lax.fori_loop(0, LOCAL // 32, norm_rows, 0)
        if (l, b) == (0, 0):
            self.need((1, l))
            self.part(l, 1)
        self.need((2, l))
        normed = r.normed[l, here, :]
        r.raw[l, b, 8:, :INNER] = dot(normed, r.inner[l, 1])
        r.raw[l, b, 8:, INNER:] = dot(normed, r.state[l])
        if l == 0:
            if b == 0:
                pl.semaphore_wait(self.barrier, SEQ - 1 + HEAD - 1)
            edge = self.pass_on(l, b)
        pushed = jnp.concatenate([dot_nt(normed, r.step[l]), jnp.zeros((LOCAL, LANES - HEADS), F32)], axis=1)
        pushed = pushed + head_row(r.step_bias, l)
        sizes = jax.nn.softplus(pushed)
        r.dt[l, here, :] = sizes
        r.sig[l, here, :] = jax.nn.sigmoid(pushed)
        rows, columns = masks()
        lower = (rows >= columns).astype(F32)
        rate = -jnp.exp(head_row(r.decay_log, l))
        r.logs[l, here, :] = dot(lower, sizes * rate, HIGHEST)
        yield
        edge.wait_recv()
        values = r.halo[l, b]
        borrowed = jnp.where(place.s == 0, 0.0, values * rms_factor(values) * gain).astype(LOW)
        r.raw[l, b, 0:8, :INNER] = dot(borrowed, r.inner[l, 1])
        r.raw[l, b, 0:8, INNER:] = dot(borrowed, r.state[l])
        summed = jnp.concatenate([row(r.conv_bias, l), row(r.conv_state_bias, l)], axis=1)
        for tap in range(4):
            summed = summed + self.taps(l, tap) * r.raw[l, b, 5 + tap : 5 + tap + LOCAL, :]
        r.pre[l, here, :] = summed
        r.act[l, here, :] = (summed * jax.nn.sigmoid(summed)).astype(LOW)
        lanes = head_lanes()
        ending = r.logs[l, (b + 1) * LOCAL - 1 : (b + 1) * LOCAL, :]
        tail = dot(jnp.exp(ending - r.logs[l, here, :]) * r.dt[l, here, :], lanes, HIGHEST)
        xs, bs, cs = r.act[l, here, :INNER], r.act[l, here, INNER : INNER + STATE], r.act[l, here, INNER + STATE :]
        exchange = Exchange(place, r, l, b, False)
        exchange.start(dot_tn(two(xs.astype(F32) * tail, 0), twice(bs, 0)), self.decays(l, b))
        yield
        if (l, b) == (0, 0):
            self.part(l, 0)
            self.more_loads()
        r.gate[l, here, :] = dot(normed, r.inner[l, 0])
        scores = jnp.where(rows >= columns, dot_nt(cs, bs), 0.0)
        turned_logs = r.logs[l, here, :].T
        turned_dt = r.dt[l, here, :].T
        for p in range(HEADS // 2):
            weights = []
            for h in (2 * p, 2 * p + 1):
                fall = jnp.minimum(r.logs[l, here, h : h + 1] - turned_logs[h : h + 1, :], 0.0)
                weights.append(scores * jnp.exp(fall) * turned_dt[h : h + 1, :])
            cols = slice(p * LANES, (p + 1) * LANES)
            r.y[l, here, cols] = dot(two(jnp.concatenate(weights, axis=1), 1), twice(split_pair(xs[:, cols]), 0))
        yield
        exchange.turn()
        yield
        start = exchange.finish()
        r.s0[l, b * INNER : (b + 1) * INNER, :] = start
        grown = dot(jnp.exp(r.logs[l, here, :]), lanes, HIGHEST)
        skip = dot(head_row(r.skip_gain, l), lanes, HIGHEST)
        values = r.y[l, here, :] + dot_nt(twice(cs, 1), two(start, 1)) * grown + skip * xs.astype(F32)
        r.y[l, here, :] = values
        gates = r.gate[l, here, :]
        gated = values * (gates * jax.nn.sigmoid(gates))
        ones = jnp.ones((8, INNER), F32)
        sums = dot_nt(ones, gated * gated, HIGHEST)
        mixer = row(r.mixer_gain, l)
        self.need((4, l))
        if l == LAYERS - 1:
            self.need((5, b))
            r.grad_low[l, here, :] = r.grad[LAYERS, here, :].astype(LOW)
            dmixed = dot(r.grad_low[l, here, :], r.wout[l])
            r.dy[here, :] = dmixed
            inner_sums = dot_nt(ones, dmixed * mixer * gated, HIGHEST)
            first = lax.broadcasted_iota(jnp.int32, (8, LOCAL), 0) == 0
            sums = jnp.where(first, sums, inner_sums)
        r.sums[l, b] = sums
        r.sums_seen[l, b, place.h] = sums
        self.sums_sent[l, b] = [
            mail.copy(r.sums.at[l, b], r.sums_seen.at[l, b, place.h], place.along_head(k)) for k in range(1, HEAD)
        ]
        r.dact[here, :INNER] = gated
        yield
        self.over_head(l, b)
        r.mixed[l, here, :] = (r.dact[here, :INNER] * r.factor[l, here, :][:, :1] * mixer).astype(LOW)
        part = r.part if l < LAYERS - 1 else r.last_part
        part[here, :] = dot_nt(r.mixed[l, here, :], r.wout[l])

    def over_head(self, l, b):
        r = self.r
        for message in self.sums_sent[l, b]:
            message.wait_recv()
        sums = r.sums_seen[l, b, 0]
        for k in range(1, HEAD):
            sums = sums + r.sums_seen[l, b, k]
        columns = jnp.concatenate([sums, jnp.zeros((LOCAL - 8, LOCAL), F32)], axis=0).T
        factor = lax.rsqrt(columns[:, 0:1] / TOTAL + EPSILON)
        r.factor[l, seq_rows(b), :] = jnp.broadcast_to(factor, (LOCAL, LANES))
        r.means[seq_rows(b), :] = jnp.broadcast_to(columns[:, 1:2] * factor / TOTAL, (LOCAL, LANES))

    def forward_sum(self, l, b):
        r = self.r

        def finalize(total, mine):
            return r.res[l, mine, :] + total

        if l < LAYERS - 1:
            return self.head_summing(l, b, r.part, self.wide(), r.res.at[l + 1], finalize)
        return self.head_summing(l, b, r.last_part, self.last(), r.res.at[l + 1], finalize)

    def backward(self, l, b):
        r, place, mail = self.r, self.place, self.mail
        here = seq_rows(b)
        lanes = head_lanes()
        rows, columns = masks()
        mixer = row(r.mixer_gain, l)
        skip = dot(head_row(r.skip_gain, l), lanes, HIGHEST)
        xs, bs, cs = r.act[l, here, :INNER], r.act[l, here, INNER : INNER + STATE], r.act[l, here, INNER + STATE :]
        if l == LAYERS - 1:
            dmixed, means = r.dy[here, :], r.means[here, :][:, :1]
        else:
            low = r.grad[l + 1, here, :].astype(LOW)
            r.grad_low[l, here, :] = low
            dmixed = dot(low, r.wout[l])
            branch = r.res[l + 1, here, :] - r.res[l, here, :]
            means = jnp.sum(low.astype(F32) * branch, axis=-1, keepdims=True) / TOTAL
        factor = r.factor[l, here, :][:, :1]
        gates, values = r.gate[l, here, :], r.y[l, here, :]
        opened = jax.nn.sigmoid(gates)
        silu = gates * opened
        q = values * silu * factor
        self.add_small(l, 0, jnp.sum(dmixed * q, axis=0, keepdims=True))
        dgated = factor * (dmixed * mixer - q * means)
        dvalues = dgated * silu
        r.dy[here, :] = dvalues
        r.dproj[l, here, :INNER] = (dgated * values * opened * (1.0 + gates * (1.0 - opened))).astype(LOW)
        self.add_small(l, 3, jnp.sum(dvalues * xs.astype(F32), axis=0, keepdims=True))
        grown = dot(jnp.exp(r.logs[l, here, :]), lanes, HIGHEST)
        scaled = two(grown * dvalues, 1)
        exchange = Exchange(place, r, l, b, True)
        exchange.start(dot_tn(two(grown * dvalues, 0), twice(cs, 0)))
        yield
        inside = (rows >= columns).astype(F32)
        scores = dot_nt(cs, bs) * inside
        turned_logs = r.logs[l, here, :].T
        turned_dt = r.dt[l, here, :].T
        dscores = jnp.zeros((LOCAL, LOCAL), F32)
        row_sums, column_sums = [], []
        for p in range(HEADS // 2):
            cols = slice(p * LANES, (p + 1) * LANES)
            dys = two(split_pair(r.dy[here, cols]), 1)
            both = dot_nt(dys, twice(xs[:, cols], 1))
            weights = []
            for k in range(2):
                h = 2 * p + k
                fall = jnp.exp(jnp.minimum(r.logs[l, here, h : h + 1] - turned_logs[h : h + 1, :], 0.0))
                steps = turned_dt[h : h + 1, :]
                weights.append(scores * fall * steps)
                moved = both[k * LOCAL : (k + 1) * LOCAL] * fall
                dscores += moved * steps
                moved = moved * scores
                column_sums.append(jnp.sum(moved, axis=0, keepdims=True))
                row_sums.append(jnp.sum(moved * steps, axis=1, keepdims=True))
            weights = two(jnp.concatenate(weights, axis=0), 0)
            high, low = dys[:, :LANES], dys[:, LANES:]
            r.dact[here, cols] = dot_tn(weights, twice(high, 0)) + dot_tn(weights[:SEQS * LOCAL], low)
        dscores = dscores * inside
        start = two(r.s0[l, b * INNER : (b + 1) * INNER, :], 1)
        r.dact[here, INNER : INNER + STATE] = dot_tn(two(dscores, 0), twice(cs, 0))
        r.dact[here, INNER + STATE :] = dot(two(dscores, 1), twice(bs, 0)) + product_of_two(scaled, start)
        carried = dot_nt(twice(cs, 1), start)
        from_start = dot_nt(carried * r.dy[here, :], lanes, HIGHEST) * jnp.exp(r.logs[l, here, :])
        by_column = jnp.concatenate(column_sums + [jnp.zeros((LOCAL - HEADS, LOCAL), F32)], axis=0).T
        by_row = jnp.concatenate(row_sums + [jnp.zeros((LOCAL, LANES - HEADS), F32)], axis=1)
        r.dlogs[b, 0] = by_row - by_column * r.dt[l, here, :] + from_start
        r.dlogs[b, 1] = by_column
        yield
        exchange.turn()
        yield
        upper = (rows <= columns).astype(F32)
        strict = (rows > columns).astype(F32)
        ending = r.logs[l, (b + 1) * LOCAL - 1 : (b + 1) * LOCAL, :]
        tail = jnp.exp(ending - r.logs[l, here, :])
        tail_dt = dot(tail * r.dt[l, here, :], lanes, HIGHEST)
        ends = exchange.finish()
        ends_two = two(ends, 1)
        reach = dot_nt(twice(bs, 1), ends_two)
        xs = xs.astype(F32)
        pulled = dot_nt(xs * reach, lanes, HIGHEST) * tail
        r.dact[here, :INNER] += tail_dt * reach + skip * r.dy[here, :]
        r.dact[here, INNER : INNER + STATE] += product_of_two(two(xs * tail_dt, 1), ends_two)
        ones = jnp.ones((8, LANES), F32)
        starts = r.s0[l, b * INNER : (b + 1) * INNER, :]
        overlap = dot_nt(dot_nt(ones, ends * starts, HIGHEST), lanes, HIGHEST)[:1]
        dt = r.dt[l, here, :]
        dlas = (
            dot(upper, r.dlogs[b, 0], HIGHEST) + dot(strict, pulled * dt, HIGHEST) + overlap * jnp.exp(ending)
        )
        rate = -jnp.exp(head_row(r.decay_log, l))
        dstep = (r.dlogs[b, 1] + pulled + dlas * rate) * r.sig[l, here, :]
        r.dproj[l, here, INNER + CONV :] = dstep.astype(LOW)
        before = r.pre[l, here, :]
        opened = jax.nn.sigmoid(before)
        dbefore = r.dact[here, :] * opened * (1.0 + before * (1.0 - opened))
        r.dpre[b, 0:LOCAL, :] = dbefore
        r.edge[l, b] = dbefore[0:8]
        edge = mail.copy(r.edge.at[l, b], r.edge_seen.at[l, b], place.along_seq(-1))
        self.add_small(l, 6, jnp.sum(dstep, axis=0, keepdims=True))
        self.add_small(l, 7, jnp.sum(dlas * dt, axis=0, keepdims=True) * rate)
        self.add_small(l, 8, jnp.sum(dbefore, axis=0, keepdims=True))
        for tap in range(4):
            shifted = r.raw[l, b, 5 + tap : 5 + tap + LOCAL, :]
            self.add_small(l, 13 + 5 * tap, jnp.sum(dbefore * shifted, axis=0, keepdims=True))
        r.part[here, :] = dot_nt(r.dproj[l, here, :INNER], r.inner[l, 0]) + dot(
            r.dproj[l, here, INNER + CONV : INNER + CONV + HEADS], r.step[l]
        )
        yield
        edge.wait_recv()
        r.dpre[b, LOCAL:, :] = jnp.where(place.s == SEQ - 1, 0.0, r.edge_seen[l, b])
        draw = jnp.zeros((LOCAL, CONV), F32)
        for tap in range(4):
            draw += self.taps(l, tap) * r.dpre[b, 3 - tap : 3 - tap + LOCAL, :]
        r.dproj[l, here, INNER : INNER + CONV] = draw.astype(LOW)
        r.state_part[l, :, here] = draw[:, INNER:].T
        r.part[here, :] += dot_nt(r.dproj[l, here, INNER : 2 * INNER], r.inner[l, 1]) + dot_nt(
            r.dproj[l, here, 2 * INNER : INNER + CONV], r.state[l]
        )

    def backward_sum(self, l, b):
        r = self.r

        def finalize(dnormed, mine):
            rows = r.res[l, mine, :]
            factor = rms_factor(rows)
            u = rows * factor
            self.add_small(l, 33, jnp.sum(dnormed * u, axis=0, keepdims=True))
            du = dnormed * row(r.norm_gain, l)
            return r.grad[l + 1, mine, :] + factor * (du - u * jnp.mean(du * u, axis=-1, keepdims=True))

        return self.head_summing(l, b, r.part, self.wide(), r.grad.at[l], finalize)


    def weight_chunk(self, l, chunk):
        r, place, mail = self.r, self.place, self.mail
        own, flows = r.own, (0, 1)

        def blocks(flow, at, first, count):
            rows = pl.ds(flow * HALF + first, count)
            if flow == 0:
                return (chunk, slice(None), at, rows, slice(None))
            return (chunk, at, slice(None), rows, slice(None))

        def move(flow, steps):
            return place.along_x(steps) if flow == 0 else place.along_y(steps)

        def at_of(flow, steps):
            return place.x_at(steps) if flow == 0 else place.y_at(steps)

        def slot(flow):
            return chunk * 2 + flow

        posted = []

        def post(src, dst, to):
            posted.append(mail.copy(src, dst, to))
            return posted[-1]

        for k in range(RING):
            cols = slice(k * INNER, (k + 1) * INNER)
            if chunk == 0:
                value = dot_tn(r.grad_low[l, :, cols], r.mixed[l])
            else:
                value = dot_tn(r.normed[l, :, cols], r.dproj[l, :, (chunk - 1) * INNER : chunk * INNER])
            own[chunk, k] = value.reshape(RING, BLOCK, INNER)
        first, last = pl.ds(0, QUARTER), pl.ds(QUARTER, QUARTER)
        distant, near = {}, {}

        def parts(ref, flow, rows):
            return ref.at[slot(flow), :, rows]

        for flow in flows:
            far = at_of(flow, 2)
            distant[flow] = (
                post(own.at[blocks(flow, far, 0, QUARTER)], r.a1p.at[slot(flow)], move(flow, 1)),
                post(own.at[blocks(flow, far, QUARTER, QUARTER)], r.a1n.at[slot(flow)], move(flow, -1)),
            )
        for flow in flows:
            up, down = at_of(flow, 1), at_of(flow, -1)
            near[flow] = [
                post(own.at[blocks(flow, up, QUARTER, QUARTER)], parts(r.a2p, flow, last), move(flow, 1)),
                post(own.at[blocks(flow, down, 0, QUARTER)], parts(r.a2n, flow, first), move(flow, -1)),
            ]
        yield
        for flow in flows:
            up, down = at_of(flow, 1), at_of(flow, -1)
            for message in distant[flow]:
                message.wait_recv()
            own[blocks(flow, up, 0, QUARTER)] += r.a1p[slot(flow)]
            own[blocks(flow, down, QUARTER, QUARTER)] += r.a1n[slot(flow)]
            near[flow] += [
                post(own.at[blocks(flow, up, 0, QUARTER)], parts(r.a2p, flow, first), move(flow, 1)),
                post(own.at[blocks(flow, down, QUARTER, QUARTER)], parts(r.a2n, flow, last), move(flow, -1)),
            ]
        yield
        for flow in flows:
            k = slot(flow)
            for message in near[flow]:
                message.wait_recv()
            r.asum[k] = own[blocks(flow, at_of(flow, 0), 0, HALF)] + r.a2p[k] + r.a2n[k]
            other = 1 - flow
            far, up, down = at_of(other, 2), at_of(other, 1), at_of(other, -1)
            distant[flow] = (
                post(r.asum.at[k, far, first], r.a3p.at[k], move(other, 1)),
                post(r.asum.at[k, far, last], r.a3n.at[k], move(other, -1)),
            )
            near[flow] = [
                post(r.asum.at[k, up, last], r.a4p.at[k, last], move(other, 1)),
                post(r.asum.at[k, down, first], r.a4n.at[k, first], move(other, -1)),
            ]
        yield
        for flow in flows:
            k = slot(flow)
            other = 1 - flow
            up, down = at_of(other, 1), at_of(other, -1)
            for message in distant[flow]:
                message.wait_recv()
            r.asum[k, up, 0:QUARTER] += r.a3p[k]
            r.asum[k, down, QUARTER:HALF] += r.a3n[k]
            near[flow] += [
                post(r.asum.at[k, up, first], r.a4p.at[k, first], move(other, 1)),
                post(r.asum.at[k, down, last], r.a4n.at[k, last], move(other, -1)),
            ]
        yield
        for flow in flows:
            k = slot(flow)
            for message in near[flow]:
                message.wait_recv()
            value = r.asum[k, at_of(1 - flow, 0)] + r.a4p[k] + r.a4n[k]
            rows = slice(flow * HALF, (flow + 1) * HALF)
            if chunk == 0:
                r.output_grad[l, rows, :] = value
            else:
                r.pair_grad[l, chunk - 1, rows, :] = value
        for message in posted:
            message.done()

    def spread(self, src, dst, l, sems, slots):
        place = self.place

        def message(k):
            to = place.seq(k)
            return pltpu.make_async_remote_copy(
                src_ref=src(to) if slots is None else src.at[to] if slots else src,
                dst_ref=dst.at[place.s],
                send_sem=sems[0].at[l, k],
                recv_sem=sems[1].at[l, k],
                device_id=(to, place.h),
                device_id_type=MESH,
            )

        def each(what):
            def body(k, carry):
                what(message(k))
                return carry

            return lambda: lax.fori_loop(1, SEQ, body, 0)

        each(lambda m: m.start())()
        return each(lambda m: m.wait_recv()), each(lambda m: m.wait_send())

    def to_heads(self, src, dst, slots):
        place, mail = self.place, self.mail
        sent = []
        for k in range(1, HEAD):
            to = lax.rem(place.h + k, HEAD)
            piece = src.at[pl.ds(pl.multiple_of(to * PART, PART), PART)] if slots else src
            sent.append(mail.copy(piece, dst.at[place.h], (place.s, to)))
        return sent

    def state_weights(self, l):
        r, place = self.r, self.place
        sent = self.to_heads(r.state_part.at[l], r.state_seen.at[l], True)
        yield
        total = r.state_part[l, pl.ds(pl.multiple_of(place.h * PART, PART), PART), :]
        for k in range(1, HEAD):
            sent[k - 1].wait_recv()
        for k in range(1, HEAD):
            total = total + r.state_seen[l, lax.rem(place.h + k, HEAD)]
        steps = r.dproj[l, :, INNER + CONV :].astype(F32).T[0:8]
        both = jnp.concatenate([total, steps], axis=0).astype(LOW)
        for k in range(RING):
            product = dot(both, r.normed[l, :, k * INNER : (k + 1) * INNER])
            for j in range(RING):
                owner = k * RING + j
                r.misc[l, owner, :, 0:BLOCK] = product[:, j * BLOCK : (j + 1) * BLOCK]
        r.misc_seen[l, place.s] = r.misc[l, place.s]
        scattered = self.spread(r.misc.at[l], r.misc_seen.at[l], l, (r.scatter_send, r.scatter_recv), True)
        yield
        scattered[0]()
        total = r.misc_seen[l, 0]
        for k in range(1, SEQ):
            total = total + r.misc_seen[l, k]
        r.step_grad[l] = total[PART:]
        r.shared[l] = total[0:PART]
        r.state_grad[l, place.h] = total[0:PART]
        sent = self.to_heads(r.shared.at[l], r.shared_seen.at[l], False)
        yield
        for message in sent:
            message.wait_recv()
        for k in range(1, HEAD):
            at = lax.rem(place.h + k, HEAD)
            r.state_grad[l, at] = r.shared_seen[l, at]
        scattered[1]()

    def small_sums(self, l):
        r, place = self.r, self.place
        r.tiny_seen[l, place.s] = r.small[l, pl.ds(pl.multiple_of(place.s * SMALL_PIECE, 8), SMALL_PIECE), :]

        def piece(to):
            return r.small.at[l, pl.ds(pl.multiple_of(to * SMALL_PIECE, 8), SMALL_PIECE)]

        scattered = self.spread(piece, r.tiny_seen.at[l], l, (r.tiny_send, r.tiny_recv), None)
        yield
        scattered[0]()
        total = r.tiny_seen[l, 0]
        for k in range(1, SEQ):
            total = total + r.tiny_seen[l, k]
        r.tiny[l] = total
        sent = self.to_heads(r.tiny.at[l], r.tiny_heads.at[l], False)
        yield
        for message in sent:
            message.wait_recv()
        over_head = total
        for k in range(1, HEAD):
            over_head = over_head + r.tiny_heads[l, lax.rem(place.h + k, HEAD)]
        at = lax.broadcasted_iota(jnp.int32, (SMALL_PIECE, LANES), 0) + place.s * SMALL_PIECE
        joint = at < 0
        for low, high in SHARED:
            joint = joint | ((at >= low) & (at < high))
        r.small_seen[l, place.s] = jnp.where(joint, over_head, total)
        gathered = self.spread(
            r.small_seen.at[l, place.s], r.small_seen.at[l], l, (r.gather_send, r.gather_recv), False
        )
        yield
        gathered[0]()
        r.small_out[l] = r.small_seen[l]
        gathered[1]()
        scattered[1]()


FORWARD, FORWARD_SUM, FORWARD_DONE, BACKWARD, BACKWARD_SUM, BACKWARD_DONE = range(6)


def chain(program, b):
    for l in range(LAYERS):
        for step, _ in enumerate(program.forward(l, b)):
            yield FORWARD, l, step
        if l < LAYERS - 1:
            for step, _ in enumerate(program.forward_sum(l, b)):
                yield FORWARD_SUM, l, step
        else:
            yield FORWARD_DONE, l, 0
    for l in reversed(range(LAYERS)):
        for step, _ in enumerate(program.backward(l, b)):
            yield BACKWARD, l, step
        for step, _ in enumerate(program.backward_sum(l, b)):
            yield BACKWARD_SUM, l, step
        yield BACKWARD_DONE, l, 0


def last(b):
    return Program.forward_sum, LAYERS - 1, b


def chunk(l, k):
    return Program.weight_chunk, l, k


def state(l):
    return Program.state_weights, l


def small(l):
    return Program.small_sums, l


PART_NEXT = Program.part_next, LAYERS - 1
STORE = (Program.store,)

BEHIND = {
    (FORWARD_SUM, 0, 1, 1): (PART_NEXT,),
    (FORWARD_SUM, 0, 3, 1): (PART_NEXT,),
    (FORWARD_DONE, 1, 0, 0): (last(0),),
    (FORWARD_DONE, 1, 0, 1): (last(1),),
    (BACKWARD, 1, 0, 0): (last(0),),
    (BACKWARD, 1, 0, 1): (last(1),),
    (BACKWARD, 1, 1, 0): (last(0),),
    (BACKWARD, 1, 1, 1): (last(1),),
    (BACKWARD, 1, 2, 0): (last(0),),
    (BACKWARD, 1, 2, 1): (last(1), chunk(1, 0)),
    (BACKWARD, 1, 3, 0): (last(0),),
    (BACKWARD, 1, 3, 1): (last(1), chunk(1, 1)),
    (BACKWARD_SUM, 1, 0, 0): (last(0),),
    (BACKWARD_SUM, 1, 0, 1): (last(1), state(1), chunk(1, 0), chunk(1, 2)),
    (BACKWARD_SUM, 1, 1, 0): (last(0),),
    (BACKWARD_SUM, 1, 1, 1): (last(1), chunk(1, 1)),
    (BACKWARD_SUM, 1, 2, 1): (state(1), chunk(1, 0)),
    (BACKWARD_SUM, 1, 3, 1): (chunk(1, 1), chunk(1, 2)),
    (BACKWARD_SUM, 1, 4, 1): (chunk(1, 0),),
    (BACKWARD_SUM, 1, 5, 1): (state(1), chunk(1, 1)),
    (BACKWARD_DONE, 1, 0, 1): (STORE, chunk(1, 0), chunk(1, 2)),
    (BACKWARD, 0, 0, 1): (chunk(1, 1), chunk(1, 2)),
    (BACKWARD, 0, 1, 1): (state(1), small(1), chunk(1, 2)),
    (BACKWARD, 0, 2, 1): (chunk(0, 0),),
    (BACKWARD, 0, 3, 1): (chunk(0, 0), chunk(0, 1)),
    (BACKWARD_SUM, 0, 0, 1): (state(0), small(1), chunk(0, 0), chunk(0, 1), chunk(0, 2)),
    (BACKWARD_SUM, 0, 1, 1): (state(0), chunk(0, 1)),
    (BACKWARD_SUM, 0, 2, 1): (small(1), chunk(0, 0), chunk(0, 2)),
    (BACKWARD_SUM, 0, 3, 1): (small(0), state(0), chunk(0, 1), chunk(0, 0)),
    (BACKWARD_SUM, 0, 4, 1): (small(0), chunk(0, 2), chunk(0, 1)),
    (BACKWARD_SUM, 0, 5, 1): (small(0), state(0), small(1), chunk(0, 2)),
    (BACKWARD_DONE, 0, 0, 1): (small(0), chunk(0, 2)),
}


def whole_kernel(names, *refs):
    r = SimpleNamespace(**dict(zip(names, refs)))
    program = Program(r)
    place = program.place
    barrier = greet(
        [place.along_seq(k) for k in range(1, SEQ)] + [place.along_head(k) for k in range(1, HEAD)]
    )
    program.start_loads()
    r.small[...] = jnp.zeros_like(r.small)
    r.misc[...] = jnp.zeros_like(r.misc)
    steps = r.step_in[...].astype(F32)
    for l in range(LAYERS):
        r.step[l] = steps[:, l, :].astype(LOW)
    program.barrier = barrier
    tasks = {}

    def go_on(task):
        if task not in tasks:
            tasks[task] = task[0](program, *task[1:])
        if next(tasks[task], StopIteration) is StopIteration:
            tasks[task] = iter(())

    live = {b: chain(program, b) for b in range(SEQS)}
    while live:
        for b in list(live):
            at = next(live[b], None)
            if at is None:
                del live[b]
                continue
            for name in BEHIND.get((*at, b), ()):
                go_on(name)
    program.put(r.grad.at[0], r.hidden_grad)
    for task in list(tasks) * 8:
        go_on(task)
    for copy in program.stores:
        copy.wait()
    program.mail.finish()


def floats(*shape):
    return pltpu.VMEM(shape, F32)


def lows(*shape):
    return pltpu.VMEM(shape, LOW)


def dma(*shape):
    return pltpu.SemaphoreType.DMA(shape)


def run(args):
    inputs = dict(
        hidden_in=pl.ANY,
        cotangent_in=pl.ANY,
        norm_gain=pltpu.VMEM,
        inner_in=pl.ANY,
        state_in=pl.ANY,
        step_in=pltpu.VMEM,
        conv_weight=pltpu.VMEM,
        conv_bias=pltpu.VMEM,
        conv_state_weight=pltpu.VMEM,
        conv_state_bias=pltpu.VMEM,
        step_bias=pltpu.VMEM,
        decay_log=pltpu.VMEM,
        skip_gain=pltpu.VMEM,
        mixer_gain=pltpu.VMEM,
        output_in=pl.ANY,
    )
    outputs = dict(
        hidden_out=((SEQS, LOCAL, WIDTH), pl.ANY),
        hidden_grad=((SEQS, LOCAL, WIDTH), pl.ANY),
        pair_grad=((LAYERS, 2, BLOCK, INNER), pltpu.VMEM),
        state_grad=((LAYERS, HEAD, PART, LANES), pltpu.VMEM),
        step_grad=((LAYERS, 8, LANES), pltpu.VMEM),
        small_out=((LAYERS, SEQ, SMALL_PIECE, LANES), pltpu.VMEM),
        output_grad=((LAYERS, BLOCK, INNER), pltpu.VMEM),
    )
    flows = 2 * CHUNKS
    copies = (
        (2 * LAYERS + 2 * LAYERS) * HEAD_SUM_COPIES
        + LAYERS * SEQS * (2 + HEAD - 1)
        + 3 * LAYERS * (HEAD - 1)
        + LAYERS * flows * 12
    )
    scratch = dict(
        res=floats(LAYERS + 1, ROWS, WIDTH),
        grad=floats(LAYERS + 1, ROWS, WIDTH),
        inner=lows(LAYERS, 2, WIDTH, INNER),
        mingled=lows(WIDTH, 2, INNER),
        state=lows(LAYERS, WIDTH, 2 * STATE),
        step=lows(LAYERS, HEADS, WIDTH),
        wout=lows(LAYERS, WIDTH, INNER),
        normed=lows(LAYERS, ROWS, WIDTH),
        gate=floats(LAYERS, ROWS, INNER),
        raw=floats(LAYERS, SEQS, 8 + LOCAL, CONV),
        pre=floats(LAYERS, ROWS, CONV),
        act=lows(LAYERS, ROWS, CONV),
        dt=floats(LAYERS, ROWS, LANES),
        logs=floats(LAYERS, ROWS, LANES),
        sig=floats(LAYERS, ROWS, LANES),
        y=floats(LAYERS, ROWS, INNER),
        s0=floats(LAYERS, SEQS * INNER, STATE),
        factor=floats(LAYERS, ROWS, LANES),
        means=floats(ROWS, LANES),
        sums=floats(LAYERS, SEQS, 8, LOCAL),
        sums_seen=floats(LAYERS, SEQS, HEAD, 8, LOCAL),
        halo=floats(LAYERS, SEQS, 8, WIDTH),
        part=floats(ROWS, WIDTH),
        pair=floats(SEQS, HALVED, WIDTH),
        half_p=floats(SEQS, SHARE // 2, WIDTH),
        half_n=floats(SEQS, SHARE // 2, WIDTH),
        near_p=floats(SEQS, SHARE, WIDTH),
        near_n=floats(SEQS, SHARE, WIDTH),
        last_part=floats(ROWS, WIDTH),
        last_pair=floats(SEQS, HALVED, WIDTH),
        last_half_p=floats(SEQS, SHARE // 2, WIDTH),
        last_half_n=floats(SEQS, SHARE // 2, WIDTH),
        last_near_p=floats(SEQS, SHARE, WIDTH),
        last_near_n=floats(SEQS, SHARE, WIDTH),
        state_part=floats(LAYERS, 2 * STATE, ROWS),
        state_seen=floats(LAYERS, HEAD, PART, ROWS),
        stage=floats(SEQ, PIECE + 8, LANES),
        seen=floats(SEQ, PIECE + 8, LANES),
        kept=floats(LAYERS, SEQ, 8, LANES),
        turned=floats(SEQ, PIECE, LANES),
        back=floats(SEQ, PIECE, LANES),
        grad_low=lows(LAYERS, ROWS, WIDTH),
        mixed=lows(LAYERS, ROWS, INNER),
        dproj=lows(LAYERS, ROWS, PROJ),
        dy=floats(ROWS, INNER),
        dact=floats(ROWS, CONV),
        dlogs=floats(SEQS, 2, LOCAL, LANES),
        dpre=floats(SEQS, LOCAL + 8, CONV),
        edge=floats(LAYERS, SEQS, 8, CONV),
        edge_seen=floats(LAYERS, SEQS, 8, CONV),
        small=floats(LAYERS, SMALL, LANES),
        own=floats(CHUNKS, RING, RING, BLOCK, INNER),
        a1p=floats(flows, RING, QUARTER, INNER),
        a1n=floats(flows, RING, QUARTER, INNER),
        a2p=floats(flows, RING, HALF, INNER),
        a2n=floats(flows, RING, HALF, INNER),
        asum=floats(flows, RING, HALF, INNER),
        a3p=floats(flows, QUARTER, INNER),
        a3n=floats(flows, QUARTER, INNER),
        a4p=floats(flows, HALF, INNER),
        a4n=floats(flows, HALF, INNER),
        misc=floats(LAYERS, SEQ, MISC, LANES),
        misc_seen=floats(LAYERS, SEQ, MISC, LANES),
        shared=floats(LAYERS, PART, LANES),
        shared_seen=floats(LAYERS, HEAD, PART, LANES),
        tiny=floats(LAYERS, SMALL_PIECE, LANES),
        tiny_seen=floats(LAYERS, SEQ, SMALL_PIECE, LANES),
        tiny_heads=floats(LAYERS, HEAD, SMALL_PIECE, LANES),
        small_seen=floats(LAYERS, SEQ, SMALL_PIECE, LANES),
        mail_send=dma(copies),
        mail_recv=dma(copies),
        leg1_send=dma(SEQ),
        leg1_recv=dma(SEQ),
        leg2_send=dma(SEQ),
        leg2_recv=dma(SEQ),
        scatter_send=dma(LAYERS, SEQ),
        scatter_recv=dma(LAYERS, SEQ),
        tiny_send=dma(LAYERS, SEQ),
        tiny_recv=dma(LAYERS, SEQ),
        gather_send=dma(LAYERS, SEQ),
        gather_recv=dma(LAYERS, SEQ),
        load=dma(2 * SEQS + 3 * LAYERS),
        store=dma(2 * SEQS),
    )
    results = pl.pallas_call(
        partial(whole_kernel, list(inputs) + list(outputs) + list(scratch)),
        out_shape=[jax.ShapeDtypeStruct(shape, F32) for shape, _ in outputs.values()],
        in_specs=[pl.BlockSpec(memory_space=space) for space in inputs.values()],
        out_specs=[pl.BlockSpec(memory_space=space) for _, space in outputs.values()],
        scratch_shapes=list(scratch.values()),
        compiler_params=pltpu.CompilerParams(
            collective_id=0, has_side_effects=True, vmem_limit_bytes=VMEM_LIMIT
        ),
    )(*args)
    return SimpleNamespace(**dict(zip(outputs, results)))


def pack_kernel(
    whole_out,
    whole_grad,
    pair_in,
    state_in,
    step_in,
    small,
    output_in,
    hidden_out,
    hidden_grad,
    norm_gain,
    pair,
    state,
    step,
    conv_weight,
    conv_bias,
    conv_state_weight,
    conv_state_bias,
    step_bias,
    decay_log,
    skip_gain,
    mixer_gain,
    output,
):
    hidden_out[...] = whole_out[...]
    hidden_grad[...] = whole_grad[...]
    output[...] = output_in[...]

    def lanes(l, first, count):
        rows = [small[l, (first + k) // 8, (first + k) % 8 : (first + k) % 8 + 1, :] for k in range(count)]
        return jnp.concatenate(rows, axis=1)

    for l in range(LAYERS):
        one = slice(l, l + 1)
        for part in range(2):
            pair[l, :, part, :] = pair_in[l, part]
        columns = state_in[l].reshape(2 * STATE, LANES)
        for half in range(2):
            cols = slice(half * STATE, (half + 1) * STATE)
            state[l, :, cols] = columns[cols].T[:BLOCK]
        norm_gain[one, :] = lanes(l, 33, 12)
        for head in range(HEADS):
            step[head, one, :] = step_in[l, head : head + 1, :BLOCK]
        for tap in range(4):
            conv_weight[l, tap : tap + 1, :] = lanes(l, 13 + 5 * tap, 3)
            conv_state_weight[l, tap : tap + 1, :] = lanes(l, 16 + 5 * tap, 2)
        conv_bias[one, :] = lanes(l, 8, 3)
        conv_state_bias[one, :] = lanes(l, 11, 2)
        step_bias[one, :] = lanes(l, 6, 1)[:, :HEADS]
        decay_log[one, :] = lanes(l, 7, 1)[:, :HEADS]
        skip = dot_nt(jnp.broadcast_to(lanes(l, 3, 3), (8, INNER)), head_lanes(), HIGHEST)
        skip_gain[one, :] = skip[0:1, :HEADS]
        mixer_gain[one, :] = lanes(l, 0, 3)


def shards(*args):
    args = list(args)
    args[5] = args[5].transpose(2, 0, 1)
    out = run(args)
    big = (SEQS, LOCAL, WIDTH)
    shapes = [
        big,
        big,
        (LAYERS, WIDTH),
        (LAYERS, BLOCK, 2, INNER),
        (LAYERS, BLOCK, 2 * STATE),
        (HEADS, LAYERS, BLOCK),
        (LAYERS, 4, INNER),
        (LAYERS, INNER),
        (LAYERS, 4, 2 * STATE),
        (LAYERS, 2 * STATE),
        (LAYERS, HEADS),
        (LAYERS, HEADS),
        (LAYERS, HEADS),
        (LAYERS, INNER),
        (LAYERS, BLOCK, INNER),
    ]
    held = [pl.BlockSpec(memory_space=pltpu.VMEM)]
    packed = list(
        pl.pallas_call(
            pack_kernel,
            out_shape=[jax.ShapeDtypeStruct(shape, F32) for shape in shapes],
            in_specs=held * 7,
            out_specs=held * 15,
        )(
            out.hidden_out,
            out.hidden_grad,
            out.pair_grad,
            out.state_grad,
            out.step_grad,
            out.small_out,
            out.output_grad,
        )
    )
    packed[5] = packed[5].transpose(1, 2, 0)
    return tuple(packed)


def solution(mesh):
    heads = P(None, None, "head")
    in_specs = (
        P(None, "seq", None),
        P(None, "seq", None),
        P(),
        P(None, None, None, "head"),
        P(),
        heads,
        heads,
        P(None, "head"),
        P(),
        P(),
        P(None, "head"),
        P(None, "head"),
        P(None, "head"),
        P(None, "head"),
        heads,
    )
    out_specs = (
        P(None, "seq", None),
        P(None, "seq", None),
        P(),
        P(None, "seq", None, "head"),
        P(None, "seq", None),
        P(None, "seq", "head"),
        heads,
        P(None, "head"),
        P(),
        P(),
        P(None, "head"),
        P(None, "head"),
        P(None, "head"),
        P(None, "head"),
        P(None, "seq", "head"),
    )
    return jax.shard_map(shards, mesh=mesh, in_specs=in_specs, out_specs=out_specs, check_vma=False)
```
